512 devices in a mesh: tm: 32 (over y, x), chan: 16 (over z, core).
Axes of the slice: x: 4, y: 8, z: 8, core: 2. Of those that a mesh axis runs over, the one named last changes fastest.
Arguments:
- records: bfloat16 [1, 128, 1048576], P(None, 'chan', 'tm'), may hold values from -6 to 6
- spectral_weight: bfloat16 [2048, 2, 128, 128], P(('tm', 'chan')), may hold values from -6 to 6
- skip_weight: bfloat16 [128, 128], P('chan'), may hold values from -0.5 to 0.5
- skip_bias: float32 [128], P('chan'), may hold values from -3 to 3
Outputs:
- layer_out: bfloat16 [1, 128, 1048576], P(None, 'chan', 'tm')
The draws below stay inside these ranges and needn't reach their ends.
All inputs are finite; a program needn't handle non-finite values.
Results may differ from the reference program's by a relative error of at most 0.02.
Values may be sent and summed in bfloat16 or wider, within the bound.
No kernel may reach another device: no remote copies, remote signals or barrier semaphores. Data moves between devices by JAX's collectives and lax.ppermute only.
A program may use at most 128 MiB of HBM per device.

```python
import jax
import jax.numpy as jnp
from jax import lax

CHANNELS = 128
MODES = 2048
STEPS = 1048576
RECORDS = 1


def level_of(key, shape, cuts, least, high):
    level, own = 1.0, jax.random.fold_in(key, 6)
    for position, blocks in cuts:
        steps = jnp.exp(jax.random.uniform(jax.random.fold_in(own, position), (blocks,), jnp.float32, least / len(cuts), high / len(cuts)))
        level = level * jnp.repeat(steps, shape[position] // blocks).reshape([-1 if axis == position else 1 for axis in range(len(shape))])
    return level


def scatter_about(stream_key, extent, scale, reach, cuts=(), held_as=jnp.bfloat16):
    entries = scale * jax.random.normal(stream_key, extent, jnp.float32)
    if cuts:
        entries = entries * level_of(stream_key, extent, cuts, -0.22, 0.18)
    return jnp.clip(entries, -reach, reach).astype(held_as)


def setup_inputs(seed: int = 0) -> dict:
    key_list = jax.random.split(jax.random.key(seed), 5)
    records = scatter_about(key_list[0], (RECORDS, CHANNELS, STEPS), 1.0, 6.0, ((1, 16), (2, 32)))
    spectral_weight = scatter_about(key_list[1], (MODES, 2, CHANNELS, CHANNELS), (4 * CHANNELS * MODES // STEPS) ** -0.5, 6.0, ((0, 512),))
    skip_weight = scatter_about(key_list[2], (CHANNELS, CHANNELS), CHANNELS ** -0.5, 0.5, ((0, 16),))
    skip_bias = scatter_about(key_list[3], (CHANNELS,), 0.5, 3.0, ((0, 16),), jnp.float32)
    return dict(records=records, spectral_weight=spectral_weight, skip_weight=skip_weight, skip_bias=skip_bias)


def reference(records, spectral_weight, skip_weight, skip_bias):
    signal = records.astype(jnp.float32)
    spectrum = jnp.fft.rfft(signal, axis=2)[:, :, :MODES]
    spec_real = lax.optimization_barrier(jnp.real(spectrum).astype(jnp.float32).astype(jnp.bfloat16)).astype(jnp.float32)
    spec_imag = lax.optimization_barrier(jnp.imag(spectrum).astype(jnp.float32).astype(jnp.bfloat16)).astype(jnp.float32)
    weights = spectral_weight.astype(jnp.float32)
    w_real = weights[:, 0]
    w_imag = weights[:, 1]
    mode_pos = jnp.arange(MODES, dtype=jnp.int32)
    scaling = jnp.where(mode_pos == 0, 1.0, 2.0).astype(jnp.float32) / STEPS
    mix_real = jnp.einsum("bik,kio->bok", spec_real, w_real) - jnp.einsum("bik,kio->bok", spec_imag, w_imag)
    mix_imag = jnp.einsum("bik,kio->bok", spec_real, w_imag) + jnp.einsum("bik,kio->bok", spec_imag, w_real)
    mix_real = lax.optimization_barrier((mix_real * scaling).astype(jnp.bfloat16)).astype(jnp.float32)
    mix_imag = lax.optimization_barrier((mix_imag * scaling).astype(jnp.bfloat16)).astype(jnp.float32)

    def inverse_row(pair):
        real_row, imag_row = pair
        padded_real = jnp.pad(real_row, (0, STEPS - MODES))
        padded_imag = jnp.pad(imag_row, (0, STEPS - MODES))
        modes_full = lax.complex(padded_real, padded_imag)
        return (jnp.real(jnp.fft.ifft(modes_full)) * STEPS).astype(jnp.float32)

    row_total = mix_real.shape[0] * mix_real.shape[1]
    spectral = lax.map(inverse_row, (mix_real.reshape(row_total, MODES), mix_imag.reshape(row_total, MODES)))
    spectral = spectral.reshape(signal.shape).astype(jnp.float32)
    skip = jnp.einsum("oi,bit->bot", skip_weight.astype(jnp.float32), signal)
    total = spectral + skip + skip_bias.astype(jnp.float32)[None, :, None]
    return jax.nn.gelu(total, approximate=False).astype(jnp.bfloat16)
```

```python
import math

import jax
import jax.numpy as jnp
import numpy as np
from jax import lax
from jax.experimental import pallas as pl
from jax.experimental.pallas import tpu as pltpu
from jax.sharding import PartitionSpec as P

MODES = 2048
INNER = 512
CHUNK = 256


def tables(steps_all, time_dev):
    blocks = time_dev // INNER
    tm_count = steps_all // time_dev
    modes = np.arange(MODES, dtype=np.int64)

    def turn(positions):
        phase = positions[:, None] * modes[None, :] % steps_all
        angle = phase * (2.0 * math.pi / steps_all)
        return np.cos(angle), np.sin(angle)

    inner_cos, inner_sin = turn(np.arange(INNER, dtype=np.int64))
    chunks = MODES // CHUNK
    split = lambda a: a.reshape(INNER, chunks, CHUNK)
    forward = np.stack([split(inner_cos), split(inner_sin)], axis=2).reshape(INNER, 2 * MODES)
    inverse = np.stack([split(inner_cos), -split(inner_sin)], axis=2).reshape(INNER, 2 * MODES).T
    block_turn = np.stack(turn(np.arange(blocks, dtype=np.int64) * INNER))
    start_turn = np.stack(turn(np.arange(tm_count, dtype=np.int64) * time_dev), axis=1)
    return (
        np.ascontiguousarray(forward).astype(jnp.bfloat16),
        np.ascontiguousarray(inverse).astype(jnp.bfloat16),
        block_turn.astype(np.float32),
        start_turn.astype(np.float32),
    )


def forward_kernel(where_ref, x_ref, table_ref, block_ref, start_ref, out_ref, rows_ref):
    blocks = block_ref.shape[1]
    half = 64

    @pl.when(pl.program_id(0) == 0)
    def _():
        for pair in range(blocks // 2):
            first = x_ref[:, pl.ds(2 * pair * INNER, INNER)].astype(jnp.float32)
            second = x_ref[:, pl.ds((2 * pair + 1) * INNER, INNER)].astype(jnp.float32)
            rows_ref[pl.ds(16 * pair, 16), :] = jnp.concatenate([first, second], axis=0).astype(
                jnp.bfloat16
            )

    real = jnp.zeros((8, CHUNK), jnp.float32)
    imag = jnp.zeros((8, CHUNK), jnp.float32)
    group = 16
    for g in range(blocks // group):
        product = jnp.dot(
            rows_ref[pl.ds(g * group * 8, group * 8), :],
            table_ref[...],
            preferred_element_type=jnp.float32,
        )
        for b in range(group):
            by_cos = product[8 * b : 8 * b + 8, :CHUNK]
            by_sin = product[8 * b : 8 * b + 8, CHUNK:]
            cos_b = block_ref[0, pl.ds(g * group + b, 1), :]
            sin_b = block_ref[1, pl.ds(g * group + b, 1), :]
            real = real + (by_cos * cos_b - by_sin * sin_b)
            imag = imag + (by_cos * sin_b + by_sin * cos_b)
    cos_s = start_ref[0, 0:1, :]
    sin_s = start_ref[0, 1:2, :]
    out_real = real * cos_s - imag * sin_s
    out_imag = -(real * sin_s + imag * cos_s)
    low = lax.broadcasted_iota(jnp.int32, (8, 128), 1) < half
    for tile in range(CHUNK // 128):
        re = out_real[:, 128 * tile : 128 * tile + 128]
        im = out_imag[:, 128 * tile : 128 * tile + 128]
        out_ref[2 * tile] = jnp.where(low, re, pltpu.roll(im, half, 1)).astype(out_ref.dtype)
        out_ref[2 * tile + 1] = jnp.where(low, pltpu.roll(re, half, 1), im).astype(out_ref.dtype)


def forward(where, x, table, block_turn, start_turn):
    chan_dev, time_dev = x.shape
    blocks = time_dev // INNER
    chunks = MODES // CHUNK
    owners = MODES // 64
    return pl.pallas_call(
        forward_kernel,
        grid_spec=pltpu.PrefetchScalarGridSpec(
            num_scalar_prefetch=1,
            grid=(chunks,),
            in_specs=[
                pl.BlockSpec((chan_dev, time_dev), lambda i, w: (0, 0)),
                pl.BlockSpec((INNER, 2 * CHUNK), lambda i, w: (0, i)),
                pl.BlockSpec((2, blocks, CHUNK), lambda i, w: (0, 0, i)),
                pl.BlockSpec((1, 2, CHUNK), lambda i, w: (w[0], 0, i)),
            ],
            out_specs=pl.BlockSpec((owners // chunks, chan_dev, 128), lambda i, w: (i, 0, 0)),
            scratch_shapes=[pltpu.VMEM((blocks * chan_dev, INNER), jnp.bfloat16)],
        ),
        out_shape=jax.ShapeDtypeStruct((owners, chan_dev, 128), jnp.bfloat16),
        compiler_params=pltpu.CompilerParams(vmem_limit_bytes=24 << 20),
        cost_estimate=pl.CostEstimate(
            flops=4 * chan_dev * time_dev * MODES, bytes_accessed=6 << 20, transcendentals=0
        ),
        name="forward_modes",
    )(where, x, table, block_turn, start_turn)


def inverse_kernel(where_ref, mixed_ref, table_ref, block_ref, start_ref, out_ref, turned_ref, sum_ref):
    blocks = block_ref.shape[1]
    half = 64
    step = pl.program_id(0)
    low = lax.broadcasted_iota(jnp.int32, (8, 128), 1) < half
    reals, imags = [], []
    for tile in range(CHUNK // 128):
        even = mixed_ref[2 * tile].astype(jnp.float32)
        odd = mixed_ref[2 * tile + 1].astype(jnp.float32)
        reals.append(jnp.where(low, even, pltpu.roll(odd, half, 1)))
        imags.append(jnp.where(low, pltpu.roll(even, half, 1), odd))
    in_real = jnp.concatenate(reals, axis=1)
    in_imag = jnp.concatenate(imags, axis=1)
    cos_s = start_ref[0, 0:1, :]
    sin_s = start_ref[0, 1:2, :]
    real = in_real * cos_s - in_imag * sin_s
    imag = in_real * sin_s + in_imag * cos_s
    group = 16
    for g in range(blocks // group):
        for pair in range(group // 2):
            parts = []
            for b in (g * group + 2 * pair, g * group + 2 * pair + 1):
                cos_b = block_ref[0, pl.ds(b, 1), :]
                sin_b = block_ref[1, pl.ds(b, 1), :]
                parts.append(
                    jnp.concatenate(
                        [real * cos_b - imag * sin_b, real * sin_b + imag * cos_b], axis=1
                    )
                )
            turned_ref[pl.ds((g * group + 2 * pair) * 8, 16), :] = jnp.concatenate(
                parts, axis=0
            ).astype(jnp.bfloat16)
        rows = pl.ds(g * group * 8, group * 8)
        part = jnp.dot(turned_ref[rows, :], table_ref[...], preferred_element_type=jnp.float32)

        @pl.when(step == 0)
        def _():
            sum_ref[rows, :] = part

        @pl.when(step > 0)
        def _():
            sum_ref[rows, :] += part

    @pl.when(step == pl.num_programs(0) - 1)
    def _():
        for b in range(blocks):
            out_ref[:, pl.ds(b * INNER, INNER)] = sum_ref[pl.ds(8 * b, 8), :]


def inverse(where, mixed, table, block_turn, start_turn, time_dev):
    owners, chan_dev, _ = mixed.shape
    blocks = time_dev // INNER
    chunks = MODES // CHUNK
    return pl.pallas_call(
        inverse_kernel,
        grid_spec=pltpu.PrefetchScalarGridSpec(
            num_scalar_prefetch=1,
            grid=(chunks,),
            in_specs=[
                pl.BlockSpec((owners // chunks, chan_dev, 128), lambda i, w: (i, 0, 0)),
                pl.BlockSpec((2 * CHUNK, INNER), lambda i, w: (i, 0)),
                pl.BlockSpec((2, blocks, CHUNK), lambda i, w: (0, 0, i)),
                pl.BlockSpec((1, 2, CHUNK), lambda i, w: (w[0], 0, i)),
            ],
            out_specs=pl.BlockSpec((chan_dev, time_dev), lambda i, w: (0, 0)),
            scratch_shapes=[
                pltpu.VMEM((blocks * chan_dev, 2 * CHUNK), jnp.bfloat16),
                pltpu.VMEM((blocks * chan_dev, INNER), jnp.float32),
            ],
        ),
        out_shape=jax.ShapeDtypeStruct((chan_dev, time_dev), jnp.float32),
        compiler_params=pltpu.CompilerParams(vmem_limit_bytes=24 << 20),
        cost_estimate=pl.CostEstimate(
            flops=4 * chan_dev * time_dev * MODES, bytes_accessed=6 << 20, transcendentals=0
        ),
        name="inverse_modes",
    )(where, mixed, table, block_turn, start_turn)


def mix_kernel(where_ref, spec_ref, weight_ref, scale_ref, out_ref, turned_ref, mixed_ref):
    chan = where_ref[0]
    turned_ref[...] = spec_ref[...].astype(jnp.float32).T
    mixed_ref[...] = jnp.zeros_like(mixed_ref)
    block_modes = weight_ref.shape[0]
    for m in range(block_modes):
        re_row = turned_ref[pl.ds(chan * block_modes + m, 1), :]
        im_row = turned_ref[pl.ds(64 + chan * block_modes + m, 1), :]
        both = jnp.concatenate([re_row, im_row, jnp.zeros((6, 128), jnp.float32)], axis=0).astype(
            jnp.bfloat16
        )
        by_real = jnp.dot(both, weight_ref[m, 0], preferred_element_type=jnp.float32)
        by_imag = jnp.dot(both, weight_ref[m, 1], preferred_element_type=jnp.float32)
        mode = chan * block_modes + m
        scale = scale_ref[pl.ds(mode, 1), :]
        mixed_ref[pl.ds(mode, 1), :] = (by_real[0:1] - by_imag[1:2]) * scale
        mixed_ref[pl.ds(64 + mode, 1), :] = (by_imag[0:1] + by_real[1:2]) * scale
    out_ref[...] = mixed_ref[...].T.astype(out_ref.dtype)


def mix(chan, spec, weight, scale):
    return pl.pallas_call(
        mix_kernel,
        in_specs=[
            pl.BlockSpec(memory_space=pltpu.SMEM),
            pl.BlockSpec(memory_space=pltpu.VMEM),
            pl.BlockSpec(memory_space=pltpu.VMEM),
            pl.BlockSpec(memory_space=pltpu.VMEM),
        ],
        out_specs=pl.BlockSpec(memory_space=pltpu.VMEM),
        scratch_shapes=[pltpu.VMEM((128, 128), jnp.float32), pltpu.VMEM((128, 128), jnp.float32)],
        out_shape=jax.ShapeDtypeStruct((128, 128), jnp.bfloat16),
        compiler_params=pltpu.CompilerParams(vmem_limit_bytes=16 << 20),
        name="mix_modes",
    )(chan, spec, weight, scale)


def shards(records, spectral_weight, skip_weight, skip_bias):
    groups, chan_dev, time_dev = records.shape
    tm_count = lax.axis_size("tm")
    chan_count = lax.axis_size("chan")
    steps_all = time_dev * tm_count
    forward_table, inverse_table, block_turn, start_turn = tables(steps_all, time_dev)
    owner_modes = MODES // tm_count
    time_index = lax.axis_index("tm").astype(jnp.int32).reshape(1)
    chan_index = lax.axis_index("chan").astype(jnp.int32).reshape(1)
    x = records.reshape(chan_dev, time_dev)

    gathered = lax.all_gather(x, "chan", axis=0, tiled=True)

    partial = forward(time_index, x, forward_table, block_turn, start_turn)
    arrived = lax.all_to_all(partial, "tm", 0, 0, tiled=True)
    spectrum = jnp.sum(arrived.astype(jnp.float32), axis=0).astype(jnp.bfloat16)
    spectrum = jnp.broadcast_to(spectrum[None], (chan_count, chan_dev, 128))
    spectrum = lax.all_to_all(spectrum, "chan", 0, 0, tiled=True).reshape(128, 128)

    own = lax.axis_index("tm") * owner_modes + jnp.arange(owner_modes, dtype=jnp.int32)
    scale = jnp.where(own == 0, 1.0, 2.0).astype(jnp.float32) / steps_all
    scale = jnp.broadcast_to(scale[:, None], (owner_modes, 128))
    mixed = mix(chan_index, spectrum, spectral_weight, scale)
    mixed = lax.all_to_all(mixed.reshape(chan_count, chan_dev, 128), "chan", 0, 0, tiled=True)
    mixed = jnp.sum(mixed.astype(jnp.float32), axis=0).astype(jnp.bfloat16)
    mixed = jnp.broadcast_to(mixed[None], (tm_count, chan_dev, 128))
    mixed = lax.all_to_all(mixed, "tm", 0, 0, tiled=True)

    spectral = inverse(time_index, mixed, inverse_table, block_turn, start_turn, time_dev)
    skip = jnp.dot(skip_weight, gathered, preferred_element_type=jnp.float32)
    combined = spectral + skip + skip_bias[:, None]
    out = jax.nn.gelu(combined, approximate=False).astype(jnp.bfloat16)
    return out.reshape(groups, chan_dev, time_dev)


def solution(mesh):
    return jax.shard_map(
        shards,
        mesh=mesh,
        in_specs=(
            P(None, "chan", "tm"),
            P(("tm", "chan"), None, None, None),
            P("chan", None),
            P("chan"),
        ),
        out_specs=P(None, "chan", "tm"),
        check_vma=False,
    )
```

```python
import math

import jax
import jax.numpy as jnp
import numpy as np
from jax import lax
from jax.experimental import pallas as pl
from jax.experimental.pallas import tpu as pltpu
from jax.sharding import Mesh
from jax.sharding import PartitionSpec as P

MODES = 2048
INNER = 512
CHUNK = 256
LOW = 8
LANES = 128
OWN = 32


def mode_order(tm_count, depth, cores):
    share = MODES // (tm_count * depth * cores)
    modes = np.arange(MODES, dtype=np.int64).reshape(tm_count, depth, cores, share)
    return modes.transpose(0, 2, 1, 3).reshape(-1)


def tables(steps_all, time_dev, modes):
    tm_count = steps_all // time_dev
    blocks = time_dev // INNER

    def turn(positions):
        angle = positions[:, None] * modes[None, :] % steps_all * (2.0 * math.pi / steps_all)
        return np.cos(angle), np.sin(angle)

    inner_cos, inner_sin = turn(np.arange(INNER, dtype=np.int64))
    split = lambda a: a.reshape(INNER, MODES // CHUNK, CHUNK)
    forward = np.stack([split(inner_cos), split(inner_sin)], axis=2).reshape(INNER, 2 * MODES)
    inverse = np.stack([split(inner_cos), -split(inner_sin)], axis=2).reshape(INNER, 2 * MODES).T
    low = np.stack(turn(np.arange(LOW, dtype=np.int64) * INNER))
    high = np.stack(turn(np.arange(blocks // LOW, dtype=np.int64) * (INNER * LOW)))
    start = np.stack(turn(np.arange(tm_count, dtype=np.int64) * time_dev), axis=1)
    return (
        np.ascontiguousarray(forward).astype(jnp.bfloat16),
        np.ascontiguousarray(inverse).astype(jnp.bfloat16),
        low.astype(np.float32),
        high.astype(np.float32),
        start.astype(np.float32),
    )


def column_select(depth, cores, chan_dev):
    pick = np.zeros((cores, LANES, LANES), np.float32)
    for core in range(cores):
        for z in range(depth):
            for ch in range(chan_dev):
                pick[core, (z * cores + core) * chan_dev + ch, 64 + z * chan_dev + ch] = 1.0
    return pick.astype(jnp.bfloat16)


def lane_ids(rows):
    return lax.broadcasted_iota(jnp.int32, (rows, LANES), 1)


def transpose_kernel(w_ref, out_ref):
    for m in range(w_ref.shape[0]):
        for part in range(w_ref.shape[1]):
            out_ref[m, part] = w_ref[m, part].astype(jnp.float32).T.astype(out_ref.dtype)


def transpose_weights(weight):
    return pl.pallas_call(
        transpose_kernel,
        in_specs=[pl.BlockSpec(memory_space=pltpu.VMEM)],
        out_specs=pl.BlockSpec(memory_space=pltpu.VMEM),
        out_shape=jax.ShapeDtypeStruct(weight.shape, weight.dtype),
        name="transpose_weights",
    )(weight)


def forward_kernel(
    where_ref, x_ref, skip_ref, pick_ref, table_ref, low_ref, high_ref, start_ref, out_ref, rows_ref, picked_ref
):
    chan_dev = x_ref.shape[0]
    highs = high_ref.shape[1]
    span = LOW * chan_dev

    @pl.when(pl.program_id(0) == 0)
    def _():
        for pair in range(highs * LOW // 2):
            first = x_ref[:, pl.ds(2 * pair * INNER, INNER)].astype(jnp.float32)
            second = x_ref[:, pl.ds((2 * pair + 1) * INNER, INNER)].astype(jnp.float32)
            rows_ref[pl.ds(16 * pair, 16), :] = jnp.concatenate([first, second], axis=0).astype(
                jnp.bfloat16
            )
        for core in range(2):
            picked_ref[core] = jnp.dot(
                skip_ref[...], pick_ref[core], preferred_element_type=jnp.float32
            )

    cos_s = start_ref[0, 0:1, :]
    sin_s = start_ref[0, 1:2, :]
    high_cos = high_ref[0] * cos_s - high_ref[1] * sin_s
    high_sin = high_ref[0] * sin_s + high_ref[1] * cos_s
    real = jnp.zeros((chan_dev, CHUNK), jnp.float32)
    imag = jnp.zeros((chan_dev, CHUNK), jnp.float32)
    product = jnp.dot(rows_ref[...], table_ref[...], preferred_element_type=jnp.float32)
    for h in range(highs):
        part_real = jnp.zeros((chan_dev, CHUNK), jnp.float32)
        part_imag = jnp.zeros((chan_dev, CHUNK), jnp.float32)
        for b in range(LOW):
            row = h * span + b * chan_dev
            by_cos = product[row : row + chan_dev, :CHUNK]
            by_sin = product[row : row + chan_dev, CHUNK:]
            cos_b = low_ref[0, b : b + 1, :]
            sin_b = low_ref[1, b : b + 1, :]
            part_real = part_real + (by_cos * cos_b - by_sin * sin_b)
            part_imag = part_imag + (by_cos * sin_b + by_sin * cos_b)
        cos_h = high_cos[h : h + 1]
        sin_h = high_sin[h : h + 1]
        real = real + (part_real * cos_h - part_imag * sin_h)
        imag = imag - (part_real * sin_h + part_imag * cos_h)
    lane = lane_ids(chan_dev)
    for tile in range(CHUNK // LANES):
        re = real[:, LANES * tile : LANES * (tile + 1)]
        im = imag[:, LANES * tile : LANES * (tile + 1)]
        for q in range(LANES // OWN):
            re_q = pltpu.roll(re, (LANES - OWN * q) % LANES, 1) if q else re
            im_q = pltpu.roll(im, (OWN - OWN * q) % LANES, 1) if q != 1 else im
            own = jnp.where(lane < OWN, re_q, im_q)
            own = jnp.where(lane < 2 * OWN, own, picked_ref[q % 2])
            out_ref[4 * tile + q] = own.astype(out_ref.dtype)


def forward(where, x, skip_weight, pick, table, low, high, start):
    chan_dev, time_dev = x.shape
    chunks = MODES // CHUNK
    owners = MODES // OWN
    whole = lambda a: pl.BlockSpec(a.shape, lambda i, w: (0,) * a.ndim)
    return pl.pallas_call(
        forward_kernel,
        grid_spec=pltpu.PrefetchScalarGridSpec(
            num_scalar_prefetch=1,
            grid=(chunks,),
            in_specs=[
                whole(x),
                whole(skip_weight),
                whole(pick),
                pl.BlockSpec((INNER, 2 * CHUNK), lambda i, w: (0, i)),
                pl.BlockSpec((2, LOW, CHUNK), lambda i, w: (0, 0, i)),
                pl.BlockSpec((2, high.shape[1], CHUNK), lambda i, w: (0, 0, i)),
                pl.BlockSpec((1, 2, CHUNK), lambda i, w: (w[0], 0, i)),
            ],
            out_specs=pl.BlockSpec((owners // chunks, chan_dev, LANES), lambda i, w: (i, 0, 0)),
            scratch_shapes=[
                pltpu.VMEM((time_dev // INNER * chan_dev, INNER), jnp.bfloat16),
                pltpu.VMEM((2, chan_dev, LANES), jnp.float32),
            ],
        ),
        out_shape=jax.ShapeDtypeStruct((owners, chan_dev, LANES), jnp.bfloat16),
        cost_estimate=pl.CostEstimate(
            flops=4 * chan_dev * time_dev * MODES, bytes_accessed=6 << 20, transcendentals=0
        ),
        name="forward_modes",
    )(where, x, skip_weight, pick, table, low, high, start)


def sum_kernel(arrived_ref, spec_ref, skip_ref):
    owners = arrived_ref.shape[0]
    lane = lane_ids(arrived_ref.shape[1])
    sums, skips = [], []
    for core in range(2):
        total = arrived_ref[core].astype(jnp.float32)
        skips.append(pltpu.roll(total, 64, 1))
        for sender in range(2 + core, owners, 2):
            total = total + arrived_ref[sender].astype(jnp.float32)
        sums.append(total)
    both = jnp.where(lane < 64, sums[0], pltpu.roll(sums[1], 64, 1)).astype(spec_ref.dtype)
    for z in range(spec_ref.shape[0]):
        spec_ref[z] = both
    skip_ref[...] = jnp.concatenate(skips, axis=0).astype(skip_ref.dtype)


def sum_spectra(arrived, depth):
    _, chan_dev, _ = arrived.shape
    return pl.pallas_call(
        sum_kernel,
        in_specs=[pl.BlockSpec(memory_space=pltpu.VMEM)],
        out_specs=[pl.BlockSpec(memory_space=pltpu.VMEM)] * 2,
        out_shape=[
            jax.ShapeDtypeStruct((depth, chan_dev, LANES), jnp.bfloat16),
            jax.ShapeDtypeStruct((2 * chan_dev, LANES), jnp.bfloat16),
        ],
        compiler_params=pltpu.CompilerParams(vmem_limit_bytes=8 << 20),
        name="sum_spectra",
    )(arrived)


def mix_kernel(where_ref, spec_ref, weight_ref, out_ref, held_ref, sem, *, steps_all):
    depth, share, _, outs, _ = held_ref.shape
    copy = pltpu.make_async_copy(
        weight_ref.at[:, :, :, pl.ds(pl.multiple_of(where_ref[0] * outs, outs), outs), :], held_ref, sem
    )
    copy.start()
    rows = []
    for z in range(depth):
        both = spec_ref[z].astype(jnp.float32)
        rows += [both, pltpu.roll(both, 64, 1)]
    spec = jnp.concatenate(rows, axis=0).astype(jnp.bfloat16)
    lane = lane_ids(outs)
    copy.wait()
    by_real = jnp.zeros((outs, LANES), jnp.float32)
    by_imag = jnp.zeros((outs, LANES), jnp.float32)
    for z in range(depth):
        held = held_ref[z].reshape(share * 2 * outs, LANES)
        product = jnp.dot(held, spec, preferred_element_type=jnp.float32)
        for m in range(share):
            here = lane % OWN == z * share + m
            row = 2 * m * outs
            by_real = jnp.where(here, product[row : row + outs], by_real)
            by_imag = jnp.where(here, product[row + outs : row + 2 * outs], by_imag)
    mixed = by_real + jnp.where(
        lane < OWN, -pltpu.roll(by_imag, LANES - OWN, 1), pltpu.roll(by_imag, OWN, 1)
    )
    zero_mode = (lane % OWN == 0) & (where_ref[1] == 0)
    mixed = mixed * jnp.where(zero_mode, 1.0 / steps_all, 2.0 / steps_all)
    half = outs // 2
    for core in range(2):
        part = mixed[core * half : (core + 1) * half].astype(out_ref.dtype)
        for p in range(out_ref.shape[0] // 2):
            out_ref[2 * p + core] = part


def mix(where, spec, weight, owners, steps_all):
    depth, chan_dev, _ = spec.shape
    share = weight.shape[1]
    return pl.pallas_call(
        lambda *refs: mix_kernel(*refs, steps_all=steps_all),
        in_specs=[
            pl.BlockSpec(memory_space=pltpu.SMEM),
            pl.BlockSpec(memory_space=pltpu.VMEM),
            pl.BlockSpec(memory_space=pltpu.HBM),
        ],
        out_specs=pl.BlockSpec(memory_space=pltpu.VMEM),
        scratch_shapes=[
            pltpu.VMEM((depth, share, 2, 2 * chan_dev, LANES), jnp.bfloat16),
            pltpu.SemaphoreType.DMA,
        ],
        out_shape=jax.ShapeDtypeStruct((owners, chan_dev, LANES), jnp.bfloat16),
        compiler_params=pltpu.CompilerParams(vmem_limit_bytes=8 << 20),
        name="mix_modes",
    )(where, spec, weight)


def skip_kernel(core_ref, weight_ref, x_ref, own_ref, other_ref):
    inputs, width = x_ref.shape
    quarter = width // 4
    weight = weight_ref[...].astype(jnp.float32)
    low = lane_ids(16) < 64
    first = jnp.where(low, weight, 0.0)
    second = pltpu.roll(first, 64, 1)
    none = jnp.zeros_like(first)
    stacked = jnp.concatenate(
        [
            jnp.concatenate([first, none], axis=1),
            jnp.concatenate([second, none], axis=1),
            jnp.concatenate([none, first], axis=1),
            jnp.concatenate([none, second], axis=1),
        ],
        axis=0,
    ).astype(jnp.bfloat16)
    x = jnp.concatenate([x_ref[:, q * quarter : (q + 1) * quarter] for q in range(4)], axis=0)
    product = jnp.dot(stacked, x, preferred_element_type=jnp.float32)
    is_first = core_ref[0] == 0
    for q in range(4):
        core0 = product[16 * q : 16 * q + 8]
        core1 = product[16 * q + 8 : 16 * q + 16]
        own_ref[:, q * quarter : (q + 1) * quarter] = jnp.where(is_first, core0, core1)
        other_ref[:, q * quarter : (q + 1) * quarter] = jnp.where(is_first, core1, core0).astype(
            other_ref.dtype
        )


def skip_parts(core, weight, x):
    inputs, time_dev = x.shape
    width = 4096
    return pl.pallas_call(
        skip_kernel,
        grid=(time_dev // width,),
        in_specs=[
            pl.BlockSpec(memory_space=pltpu.SMEM),
            pl.BlockSpec(weight.shape, lambda i: (0, 0)),
            pl.BlockSpec((inputs, width), lambda i: (0, i)),
        ],
        out_specs=[pl.BlockSpec((8, width), lambda i: (0, i))] * 2,
        out_shape=[
            jax.ShapeDtypeStruct((8, time_dev), jnp.float32),
            jax.ShapeDtypeStruct((8, time_dev), jnp.bfloat16),
        ],
        cost_estimate=pl.CostEstimate(
            flops=2 * 16 * inputs * time_dev, bytes_accessed=6 << 20, transcendentals=0
        ),
        name="skip_parts",
    )(core, weight, x)


def inverse_kernel(
    where_ref,
    mixed_ref,
    table_ref,
    low_ref,
    high_ref,
    start_ref,
    own_ref,
    other_ref,
    bias_ref,
    out_ref,
    turned_ref,
    sum_ref,
):
    chan_dev = own_ref.shape[0]
    highs = high_ref.shape[1]
    span = LOW * chan_dev
    step = pl.program_id(0)
    lane = lane_ids(chan_dev)
    reals, imags = [], []
    for tile in range(CHUNK // LANES):
        re = im = None
        for q in range(LANES // OWN):
            block = mixed_ref[4 * tile + q].astype(jnp.float32)
            re_q = pltpu.roll(block, OWN * q, 1) if q else block
            im_q = pltpu.roll(block, (OWN * q - OWN) % LANES, 1) if q != 1 else block
            re = re_q if q == 0 else jnp.where(lane // OWN == q, re_q, re)
            im = im_q if q == 0 else jnp.where(lane // OWN == q, im_q, im)
        reals.append(re)
        imags.append(im)
    real = jnp.concatenate(reals, axis=1)
    imag = jnp.concatenate(imags, axis=1)
    cos_s = start_ref[0, 0:1, :]
    sin_s = start_ref[0, 1:2, :]
    high_cos = high_ref[0] * cos_s - high_ref[1] * sin_s
    high_sin = high_ref[0] * sin_s + high_ref[1] * cos_s
    for h in range(highs):
        cos_h = high_cos[h : h + 1]
        sin_h = high_sin[h : h + 1]
        real_h = real * cos_h - imag * sin_h
        imag_h = real * sin_h + imag * cos_h
        for pair in range(LOW // 2):
            parts = []
            for b in (2 * pair, 2 * pair + 1):
                cos_b = low_ref[0, b : b + 1, :]
                sin_b = low_ref[1, b : b + 1, :]
                parts.append(
                    jnp.concatenate(
                        [real_h * cos_b - imag_h * sin_b, real_h * sin_b + imag_h * cos_b], axis=1
                    )
                )
            turned_ref[pl.ds(h * span + 2 * pair * chan_dev, 2 * chan_dev), :] = jnp.concatenate(
                parts, axis=0
            ).astype(jnp.bfloat16)
    product = jnp.dot(turned_ref[...], table_ref[...], preferred_element_type=jnp.float32)

    @pl.when(step == 0)
    def _():
        sum_ref[...] = product

    @pl.when(step > 0)
    def _():
        sum_ref[...] += product

    @pl.when(step == pl.num_programs(0) - 1)
    def _():
        bias = bias_ref[...][:, :1]
        for b in range(highs * LOW):
            cols = pl.ds(b * INNER, INNER)
            total = sum_ref[pl.ds(b * chan_dev, chan_dev), :] + (
                own_ref[:, cols] + other_ref[:, cols].astype(jnp.float32)
            )
            total = total + bias
            gelu = 0.5 * total * (1.0 + lax.erf(total * math.sqrt(0.5)))
            out_ref[:, cols] = gelu.astype(out_ref.dtype)


def inverse(where, mixed, table, low, high, start, own, other, bias):
    owners, chan_dev, _ = mixed.shape
    time_dev = own.shape[1]
    chunks = MODES // CHUNK
    rows = time_dev // INNER * chan_dev
    whole = lambda a: pl.BlockSpec(a.shape, lambda i, w: (0,) * a.ndim)
    return pl.pallas_call(
        inverse_kernel,
        grid_spec=pltpu.PrefetchScalarGridSpec(
            num_scalar_prefetch=1,
            grid=(chunks,),
            in_specs=[
                pl.BlockSpec((owners // chunks, chan_dev, LANES), lambda i, w: (i, 0, 0)),
                pl.BlockSpec((2 * CHUNK, INNER), lambda i, w: (i, 0)),
                pl.BlockSpec((2, LOW, CHUNK), lambda i, w: (0, 0, i)),
                pl.BlockSpec((2, high.shape[1], CHUNK), lambda i, w: (0, 0, i)),
                pl.BlockSpec((1, 2, CHUNK), lambda i, w: (w[0], 0, i)),
                whole(own),
                whole(other),
                whole(bias),
            ],
            out_specs=pl.BlockSpec((chan_dev, time_dev), lambda i, w: (0, 0)),
            scratch_shapes=[
                pltpu.VMEM((rows, 2 * CHUNK), jnp.bfloat16),
                pltpu.VMEM((rows, INNER), jnp.float32),
            ],
        ),
        out_shape=jax.ShapeDtypeStruct((chan_dev, time_dev), jnp.bfloat16),
        cost_estimate=pl.CostEstimate(
            flops=4 * chan_dev * time_dev * MODES, bytes_accessed=6 << 20, transcendentals=0
        ),
        name="inverse_modes",
    )(where, mixed, table, low, high, start, own, other, bias)


def shards(records, spectral_weight, skip_weight, skip_bias):
    groups, chan_dev, time_dev = records.shape
    tm_count = lax.axis_size(("y", "x"))
    depth = lax.axis_size("z")
    cores = lax.axis_size("core")
    steps_all = time_dev * tm_count
    modes = mode_order(tm_count, depth, cores)
    forward_table, inverse_table, low, high, start = tables(steps_all, time_dev, modes)
    pick = column_select(depth, cores, chan_dev)
    time_index = lax.axis_index(("y", "x")).astype(jnp.int32)
    core_index = lax.axis_index("core").astype(jnp.int32)
    z_index = lax.axis_index("z").astype(jnp.int32)
    x = records.reshape(chan_dev, time_dev)

    turned, x_late = lax.optimization_barrier((transpose_weights(spectral_weight), x))
    weights = lax.all_gather(turned, "z", axis=0, tiled=False)
    gathered = lax.all_gather(x_late, "z", axis=0, tiled=True)

    where = time_index.reshape(1)
    partial = forward(where, x, skip_weight, pick, forward_table, low, high, start)
    arrived = lax.all_to_all(partial, ("y", "x", "core"), 0, 0, tiled=True)
    spectrum, skip_rows = sum_spectra(arrived, depth)
    spectrum = lax.all_to_all(spectrum, "z", 0, 0, tiled=True)
    mix_where = jnp.stack([z_index, time_index * cores + core_index])
    mixed = mix(mix_where, spectrum, weights, tm_count * cores, steps_all)
    skip_rows, mixed = lax.optimization_barrier((skip_rows, mixed))
    mixed = lax.all_to_all(mixed, ("y", "x", "core"), 0, 0, tiled=True)

    own, other = skip_parts(core_index.reshape(1), skip_rows, gathered)
    other = lax.ppermute(other, "core", [(0, 1), (1, 0)])
    bias = jnp.broadcast_to(skip_bias[:, None], (chan_dev, LANES))
    out = inverse(where, mixed, inverse_table, low, high, start, own, other, bias)
    return out.reshape(groups, chan_dev, time_dev)


def solution(mesh):
    fine = Mesh(mesh.devices.reshape(8, 4, 8, 2), ("y", "x", "z", "core"))
    return jax.shard_map(
        shards,
        mesh=fine,
        in_specs=(
            P(None, ("z", "core"), ("y", "x")),
            P(("y", "x", "z", "core"), None, None, None),
            P(("z", "core"), None),
            P(("z", "core")),
        ),
        out_specs=P(None, ("z", "core"), ("y", "x")),
        check_vma=False,
    )
```

```python
import math

import jax
import jax.numpy as jnp
import numpy as np
from jax import lax
from jax.experimental import pallas as pl
from jax.experimental.pallas import tpu as pltpu
from jax.sharding import PartitionSpec as P

MODES = 2048
INNER = 512
CHUNK = 256
CHUNKS = MODES // CHUNK
LOW = 8
LANES = 128
HALF = 64
VMEM_LIMIT = 52 << 20


def tables(steps_all, time_dev):
    tm_count = steps_all // time_dev
    blocks = time_dev // INNER
    modes = np.arange(MODES, dtype=np.int64)

    def turn(positions):
        angle = positions[:, None] * modes[None, :] % steps_all * (2.0 * math.pi / steps_all)
        return np.cos(angle), np.sin(angle)

    inner_cos, inner_sin = turn(np.arange(INNER, dtype=np.int64))
    split = lambda a: a.reshape(INNER, CHUNKS, CHUNK).transpose(1, 0, 2)
    forward = np.concatenate([split(inner_cos), split(inner_sin)], axis=2)
    inverse = np.concatenate([split(inner_cos), -split(inner_sin)], axis=2).transpose(0, 2, 1)
    low = np.stack(turn(np.arange(LOW, dtype=np.int64) * INNER))
    high = np.stack(turn(np.arange(blocks // LOW, dtype=np.int64) * (INNER * LOW)))
    start = np.stack(turn(np.arange(tm_count, dtype=np.int64) * time_dev), axis=1)
    return (
        np.ascontiguousarray(forward).astype(jnp.bfloat16),
        np.ascontiguousarray(inverse).astype(jnp.bfloat16),
        low.astype(np.float32),
        high.astype(np.float32),
        start.astype(np.float32),
    )


def lane_ids(rows):
    return lax.broadcasted_iota(jnp.int32, (rows, LANES), 1)


def start_copies(pairs, sems):
    copies = [pltpu.make_async_copy(src, dst, sems.at[n]) for n, (src, dst) in enumerate(pairs)]
    for copy in copies:
        copy.start()
    return copies


def high_turns(high, start):
    cos_s, sin_s = start[0:1], start[1:2]
    return high[0] * cos_s - high[1] * sin_s, high[0] * sin_s + high[1] * cos_s


def forward_kernel(
    where_ref, x_hbm, table_hbm, low_hbm, high_hbm, start_hbm, out_ref,
    x_ref, table_ref, low_ref, high_ref, start_ref, rows_ref, product_ref, sems,
):
    chan_dev = x_ref.shape[0]
    highs = high_ref.shape[1]
    span = LOW * chan_dev
    time_dev = x_ref.shape[1]
    pieces = 4
    piece = time_dev // pieces
    pairs = [
        (x_hbm.at[:, pl.ds(n * piece, piece)], x_ref.at[:, pl.ds(n * piece, piece)])
        for n in range(pieces)
    ]
    pairs += [(table_hbm.at[0], table_ref.at[0])]
    pairs += [(low_hbm, low_ref), (high_hbm, high_ref), (start_hbm.at[where_ref[0]], start_ref)]
    pairs += [(table_hbm.at[n], table_ref.at[n]) for n in range(1, CHUNKS)]
    copies = start_copies(pairs, sems)
    for n in range(pieces):
        copies[n].wait()
        for pair in range(n * piece // INNER // 2, (n + 1) * piece // INNER // 2):
            first = x_ref[:, pl.ds(2 * pair * INNER, INNER)].astype(jnp.float32)
            second = x_ref[:, pl.ds((2 * pair + 1) * INNER, INNER)].astype(jnp.float32)
            rows_ref[pl.ds(16 * pair, 16), :] = jnp.concatenate([first, second], axis=0).astype(
                jnp.bfloat16
            )
    lane = lane_ids(chan_dev)

    def multiply(n):
        copies[pieces if n == 0 else pieces + 3 + n].wait()
        product_ref[n % 2] = jnp.dot(
            rows_ref[...], table_ref[n], preferred_element_type=jnp.float32
        )

    multiply(0)
    for copy in copies[pieces + 1 : pieces + 4]:
        copy.wait()
    for n in range(CHUNKS):
        if n + 1 < CHUNKS:
            multiply(n + 1)
        chunk = pl.ds(n * CHUNK, CHUNK)
        high_cos, high_sin = high_turns(high_ref[:, :, chunk], start_ref[:, chunk])
        for tile in range(CHUNK // LANES):
            cols = pl.ds(tile * LANES, LANES)
            sin_cols = pl.ds(CHUNK + tile * LANES, LANES)
            lanes = pl.ds(n * CHUNK + tile * LANES, LANES)
            low_cos = [low_ref[0, pl.ds(b, 1), lanes] for b in range(LOW)]
            low_sin = [low_ref[1, pl.ds(b, 1), lanes] for b in range(LOW)]
            real = imag = None
            for h in range(highs):
                part_real = part_imag = None
                for b in range(LOW):
                    rows = pl.ds(h * span + b * chan_dev, chan_dev)
                    by_cos = product_ref[n % 2, rows, cols]
                    by_sin = product_ref[n % 2, rows, sin_cols]
                    re = by_cos * low_cos[b] - by_sin * low_sin[b]
                    im = by_cos * low_sin[b] + by_sin * low_cos[b]
                    part_real = re if b == 0 else part_real + re
                    part_imag = im if b == 0 else part_imag + im
                cos_h = high_cos[h : h + 1, tile * LANES : (tile + 1) * LANES]
                sin_h = high_sin[h : h + 1, tile * LANES : (tile + 1) * LANES]
                re = part_real * cos_h - part_imag * sin_h
                im = part_real * sin_h + part_imag * cos_h
                real = re if h == 0 else real + re
                imag = im if h == 0 else imag + im
            imag = -imag
            owner = (n * CHUNK + tile * LANES) // HALF
            out_ref[owner] = jnp.where(lane < HALF, real, pltpu.roll(imag, HALF, 1)).astype(
                out_ref.dtype
            )
            out_ref[owner + 1] = jnp.where(lane < HALF, pltpu.roll(real, HALF, 1), imag).astype(
                out_ref.dtype
            )


def forward(where, x, table, low, high, start):
    chan_dev, time_dev = x.shape
    hbm = pl.BlockSpec(memory_space=pltpu.HBM)
    return pl.pallas_call(
        forward_kernel,
        in_specs=[pl.BlockSpec(memory_space=pltpu.SMEM)] + [hbm] * 5,
        out_specs=pl.BlockSpec(memory_space=pltpu.VMEM),
        scratch_shapes=[
            pltpu.VMEM(x.shape, x.dtype),
            pltpu.VMEM(table.shape, table.dtype),
            pltpu.VMEM(low.shape, low.dtype),
            pltpu.VMEM(high.shape, high.dtype),
            pltpu.VMEM(start.shape[1:], start.dtype),
            pltpu.VMEM((time_dev // INNER * chan_dev, INNER), jnp.bfloat16),
            pltpu.VMEM((2, time_dev // INNER * chan_dev, 2 * CHUNK), jnp.float32),
            pltpu.SemaphoreType.DMA((CHUNKS + 7,)),
        ],
        out_shape=jax.ShapeDtypeStruct((MODES // HALF, chan_dev, LANES), jnp.bfloat16),
        cost_estimate=pl.CostEstimate(
            flops=4 * chan_dev * time_dev * MODES, bytes_accessed=6 << 20, transcendentals=0
        ),
        name="forward_modes",
    )(where, x, table, low, high, start)


def inverse_kernel(
    where_ref, mixed_ref, table_hbm, low_hbm, high_hbm, start_hbm, out_ref,
    table_ref, low_ref, high_ref, start_ref, turned_ref, sum_ref, sems,
):
    chan_dev = mixed_ref.shape[1]
    highs = high_ref.shape[1]
    span = LOW * chan_dev
    pairs = [(low_hbm, low_ref), (high_hbm, high_ref), (start_hbm.at[where_ref[0]], start_ref)]
    pairs += [(table_hbm.at[n], table_ref.at[n]) for n in range(CHUNKS)]
    copies = start_copies(pairs, sems)
    lane = lane_ids(chan_dev)
    for copy in copies[:3]:
        copy.wait()

    def turn(n):
        chunk = pl.ds(n * CHUNK, CHUNK)
        high_cos, high_sin = high_turns(high_ref[:, :, chunk], start_ref[:, chunk])
        for tile in range(CHUNK // LANES):
            lanes = pl.ds(n * CHUNK + tile * LANES, LANES)
            owner = (n * CHUNK + tile * LANES) // HALF
            even = mixed_ref[owner].astype(jnp.float32)
            odd = mixed_ref[owner + 1].astype(jnp.float32)
            real = jnp.where(lane < HALF, even, pltpu.roll(odd, HALF, 1))
            imag = jnp.where(lane < HALF, pltpu.roll(even, HALF, 1), odd)
            low_cos = [low_ref[0, pl.ds(b, 1), lanes] for b in range(LOW)]
            low_sin = [low_ref[1, pl.ds(b, 1), lanes] for b in range(LOW)]
            for h in range(highs):
                cos_h = high_cos[h : h + 1, tile * LANES : (tile + 1) * LANES]
                sin_h = high_sin[h : h + 1, tile * LANES : (tile + 1) * LANES]
                real_h = real * cos_h - imag * sin_h
                imag_h = real * sin_h + imag * cos_h
                for b in range(0, LOW, 2):
                    rows = pl.ds(h * span + b * chan_dev, 2 * chan_dev)
                    re = [real_h * low_cos[c] - imag_h * low_sin[c] for c in (b, b + 1)]
                    im = [real_h * low_sin[c] + imag_h * low_cos[c] for c in (b, b + 1)]
                    turned_ref[n % 2, rows, pl.ds(tile * LANES, LANES)] = jnp.concatenate(
                        re, axis=0
                    ).astype(jnp.bfloat16)
                    turned_ref[n % 2, rows, pl.ds(CHUNK + tile * LANES, LANES)] = jnp.concatenate(
                        im, axis=0
                    ).astype(jnp.bfloat16)

    turn(0)
    for n in range(CHUNKS):
        copies[3 + n].wait()
        product = jnp.dot(turned_ref[n % 2], table_ref[n], preferred_element_type=jnp.float32)
        if n == 0:
            sum_ref[...] = product
        elif n + 1 < CHUNKS:
            sum_ref[...] += product
        else:
            for b in range(highs * LOW):
                rows = slice(b * chan_dev, (b + 1) * chan_dev)
                out_ref[:, pl.ds(b * INNER, INNER)] = sum_ref[rows, :] + product[rows, :]
        if n + 1 < CHUNKS:
            turn(n + 1)


def inverse(where, mixed, table, low, high, start, time_dev):
    owners, chan_dev, _ = mixed.shape
    rows = time_dev // INNER * chan_dev
    hbm = pl.BlockSpec(memory_space=pltpu.HBM)
    return pl.pallas_call(
        inverse_kernel,
        in_specs=[pl.BlockSpec(memory_space=pltpu.SMEM), pl.BlockSpec(memory_space=pltpu.VMEM)]
        + [hbm] * 4,
        out_specs=pl.BlockSpec(memory_space=pltpu.VMEM),
        scratch_shapes=[
            pltpu.VMEM(table.shape, table.dtype),
            pltpu.VMEM(low.shape, low.dtype),
            pltpu.VMEM(high.shape, high.dtype),
            pltpu.VMEM(start.shape[1:], start.dtype),
            pltpu.VMEM((2, rows, 2 * CHUNK), jnp.bfloat16),
            pltpu.VMEM((rows, INNER), jnp.float32),
            pltpu.SemaphoreType.DMA((CHUNKS + 3,)),
        ],
        out_shape=jax.ShapeDtypeStruct((chan_dev, time_dev), jnp.float32),
        compiler_params=pltpu.CompilerParams(vmem_limit_bytes=VMEM_LIMIT),
        cost_estimate=pl.CostEstimate(
            flops=4 * chan_dev * time_dev * MODES, bytes_accessed=6 << 20, transcendentals=0
        ),
        name="inverse_modes",
    )(where, mixed, table, low, high, start)


def sum_kernel(arrived_ref, out_ref):
    total = arrived_ref[0].astype(jnp.float32)
    for sender in range(1, arrived_ref.shape[0]):
        total = total + arrived_ref[sender].astype(jnp.float32)
    total = total.astype(out_ref.dtype)
    for receiver in range(out_ref.shape[0]):
        out_ref[receiver] = total


def sum_and_copy(arrived, copies):
    return pl.pallas_call(
        sum_kernel,
        in_specs=[pl.BlockSpec(memory_space=pltpu.VMEM)],
        out_specs=pl.BlockSpec(memory_space=pltpu.VMEM),
        out_shape=jax.ShapeDtypeStruct((copies, *arrived.shape[1:]), jnp.bfloat16),
        compiler_params=pltpu.CompilerParams(vmem_limit_bytes=4 << 20),
        name="sum_and_copy",
    )(arrived)


def mix_kernel(where_ref, spec_ref, weight_ref, out_ref, turned_ref, mixed_ref, *, steps_all):
    chan = where_ref[0]
    spec = jnp.concatenate([spec_ref[c].astype(jnp.float32) for c in range(spec_ref.shape[0])], axis=0)
    turned_ref[...] = spec.T
    mixed_ref[...] = jnp.zeros_like(mixed_ref)
    block_modes = weight_ref.shape[0]
    for m in range(block_modes):
        mode = chan * block_modes + m
        re_row = turned_ref[pl.ds(mode, 1), :]
        im_row = turned_ref[pl.ds(HALF + mode, 1), :]
        both = jnp.concatenate([re_row, im_row, jnp.zeros((6, LANES), jnp.float32)], axis=0).astype(
            jnp.bfloat16
        )
        by_real = jnp.dot(both, weight_ref[m, 0], preferred_element_type=jnp.float32)
        by_imag = jnp.dot(both, weight_ref[m, 1], preferred_element_type=jnp.float32)
        scale = jnp.where(where_ref[1] * HALF + mode == 0, 1.0 / steps_all, 2.0 / steps_all)
        mixed_ref[pl.ds(mode, 1), :] = (by_real[0:1] - by_imag[1:2]) * scale
        mixed_ref[pl.ds(HALF + mode, 1), :] = (by_imag[0:1] + by_real[1:2]) * scale
    mixed = mixed_ref[...].T.astype(out_ref.dtype)
    rows = out_ref.shape[1]
    for c in range(out_ref.shape[0]):
        out_ref[c] = mixed[c * rows : (c + 1) * rows]


def mix(where, spec, weight, steps_all):
    return pl.pallas_call(
        lambda *refs: mix_kernel(*refs, steps_all=steps_all),
        in_specs=[
            pl.BlockSpec(memory_space=pltpu.SMEM),
            pl.BlockSpec(memory_space=pltpu.VMEM),
            pl.BlockSpec(memory_space=pltpu.VMEM),
        ],
        out_specs=pl.BlockSpec(memory_space=pltpu.VMEM),
        scratch_shapes=[pltpu.VMEM((128, LANES), jnp.float32), pltpu.VMEM((128, LANES), jnp.float32)],
        out_shape=jax.ShapeDtypeStruct(spec.shape, jnp.bfloat16),
        compiler_params=pltpu.CompilerParams(vmem_limit_bytes=4 << 20),
        name="mix_modes",
    )(where, spec, weight)


def output_kernel(weight_ref, bias_ref, spectral_ref, x_hbm, out_ref, x_ref, sems):
    chan_dev, time_dev = out_ref.shape
    parts = x_ref.shape[0]
    width = time_dev // parts
    half = width // 2
    copies = start_copies(
        [(x_hbm.at[:, pl.ds(n * width, width)], x_ref.at[n]) for n in range(parts)], sems
    )
    weight = weight_ref[...].astype(jnp.float32)
    none = jnp.zeros_like(weight)
    stacked = jnp.concatenate(
        [jnp.concatenate([weight, none], axis=1), jnp.concatenate([none, weight], axis=1)], axis=0
    ).astype(jnp.bfloat16)
    bias = bias_ref[...]
    for n in range(parts):
        copies[n].wait()
        x = jnp.concatenate([x_ref[n, :, :half], x_ref[n, :, half:]], axis=0)
        skip = jnp.dot(stacked, x, preferred_element_type=jnp.float32)
        for side in range(2):
            cols = pl.ds(n * width + side * half, half)
            total = spectral_ref[:, cols] + skip[side * chan_dev : (side + 1) * chan_dev] + bias
            gelu = 0.5 * total * (1.0 + lax.erf(total * math.sqrt(0.5)))
            out_ref[:, cols] = gelu.astype(out_ref.dtype)


def output(weight, bias, spectral, x):
    chan_dev, time_dev = spectral.shape
    parts = 16
    vmem = pl.BlockSpec(memory_space=pltpu.VMEM)
    return pl.pallas_call(
        output_kernel,
        in_specs=[vmem, vmem, vmem, pl.BlockSpec(memory_space=pltpu.HBM)],
        out_specs=vmem,
        scratch_shapes=[
            pltpu.VMEM((parts, x.shape[0], time_dev // parts), x.dtype),
            pltpu.SemaphoreType.DMA((parts,)),
        ],
        out_shape=jax.ShapeDtypeStruct((chan_dev, time_dev), jnp.bfloat16),
        compiler_params=pltpu.CompilerParams(vmem_limit_bytes=VMEM_LIMIT),
        cost_estimate=pl.CostEstimate(
            flops=2 * 2 * chan_dev * x.shape[0] * time_dev, bytes_accessed=10 << 20, transcendentals=0
        ),
        name="skip_and_output",
    )(weight, bias, spectral, x)


def shards(records, spectral_weight, skip_weight, skip_bias):
    groups, chan_dev, time_dev = records.shape
    tm_count = lax.axis_size("tm")
    chan_count = lax.axis_size("chan")
    steps_all = time_dev * tm_count
    forward_table, inverse_table, low, high, start = tables(steps_all, time_dev)
    time_index = lax.axis_index("tm").astype(jnp.int32)
    chan_index = lax.axis_index("chan").astype(jnp.int32)
    where = time_index.reshape(1)
    x = records.reshape(chan_dev, time_dev)

    gathered = lax.all_gather(x, "chan", axis=0, tiled=True)

    partial = forward(where, x, forward_table, low, high, start)
    arrived = lax.all_to_all(partial, "tm", 0, 0, tiled=True)
    spectrum = sum_and_copy(arrived, chan_count)
    spectrum = lax.all_to_all(spectrum, "chan", 0, 0, tiled=True)
    mixed = mix(jnp.stack([chan_index, time_index]), spectrum, spectral_weight, steps_all)
    mixed = lax.all_to_all(mixed, "chan", 0, 0, tiled=True)
    mixed = sum_and_copy(mixed, tm_count)
    mixed = lax.all_to_all(mixed, "tm", 0, 0, tiled=True)
    spectral = inverse(where, mixed, inverse_table, low, high, start, time_dev)

    out = output(skip_weight, skip_bias[:, None], spectral, gathered)
    return out.reshape(groups, chan_dev, time_dev)


def solution(mesh):
    return jax.shard_map(
        shards,
        mesh=mesh,
        in_specs=(
            P(None, "chan", "tm"),
            P(("tm", "chan"), None, None, None),
            P("chan", None),
            P("chan"),
        ),
        out_specs=P(None, "chan", "tm"),
        check_vma=False,
    )
```

```python
import math

import jax
import jax.numpy as jnp
import numpy as np
from jax import lax
from jax.experimental import pallas as pl
from jax.experimental.pallas import tpu as pltpu
from jax.sharding import PartitionSpec as P

MODES = 2048
INNER = 512
SIDE = INNER // 2
CHUNK = 256
SPAN = 512
LOW = 8
LANES = 128
HALF = 64
VMEM_LIMIT = 52 << 20


def tables(steps_all, time_dev):
    tm_count = steps_all // time_dev
    blocks = time_dev // INNER
    modes = np.arange(MODES, dtype=np.int64)

    def turn(half_steps):
        angle = half_steps[:, None] * modes[None, :] % (2 * steps_all) * (math.pi / steps_all)
        return np.cos(angle), np.sin(angle)

    inner_cos, inner_sin = turn(2 * np.arange(SIDE, dtype=np.int64) + 1)

    def split(a, width):
        return a.reshape(SIDE, MODES // width, width).transpose(1, 0, 2)

    forward = np.concatenate([split(inner_cos, CHUNK), split(inner_sin, CHUNK)], axis=2)
    inverse = np.concatenate([split(inner_cos, SPAN), split(inner_sin, SPAN)], axis=2)
    inverse = inverse.transpose(0, 2, 1)
    low = np.stack(turn(np.arange(LOW, dtype=np.int64) * (2 * INNER) + INNER - 1))
    high = np.stack(turn(np.arange(blocks // LOW, dtype=np.int64) * (2 * INNER * LOW)))
    start = np.stack(turn(np.arange(tm_count, dtype=np.int64) * (2 * time_dev)), axis=1)
    return (
        np.ascontiguousarray(forward).astype(jnp.bfloat16),
        np.ascontiguousarray(inverse).astype(jnp.bfloat16),
        low.astype(np.float32),
        high.astype(np.float32),
        start.astype(np.float32),
    )


def lane_ids(rows):
    return lax.broadcasted_iota(jnp.int32, (rows, LANES), 1)


def mirror_matrix():
    row = lax.broadcasted_iota(jnp.int32, (SIDE, SIDE), 0)
    col = lax.broadcasted_iota(jnp.int32, (SIDE, SIDE), 1)
    return jnp.where(row + col == SIDE - 1, 1.0, 0.0).astype(jnp.bfloat16)


def start_copies(pairs, sems):
    copies = [pltpu.make_async_copy(src, dst, sems.at[n]) for n, (src, dst) in enumerate(pairs)]
    for copy in copies:
        copy.start()
    return copies


def high_turns(high, start):
    cos_s, sin_s = start[0:1], start[1:2]
    return high[0] * cos_s - high[1] * sin_s, high[0] * sin_s + high[1] * cos_s


def forward_kernel(
    where_ref, x_hbm, table_hbm, low_hbm, high_hbm, start_hbm, out_ref,
    x_ref, table_ref, low_ref, high_ref, start_ref, sum_ref, diff_ref, product_ref, sems,
):
    chan_dev, time_dev = x_ref.shape
    highs = high_ref.shape[1]
    span = LOW * chan_dev
    chunks = MODES // CHUNK
    pieces = 1
    piece = time_dev // pieces
    pairs = [
        (x_hbm.at[:, pl.ds(n * piece, piece)], x_ref.at[:, pl.ds(n * piece, piece)])
        for n in range(pieces)
    ]
    pairs += [(table_hbm.at[0], table_ref.at[0])]
    pairs += [(low_hbm, low_ref), (high_hbm, high_ref), (start_hbm.at[where_ref[0]], start_ref)]
    pairs += [(table_hbm.at[n], table_ref.at[n]) for n in range(1, chunks)]
    copies = start_copies(pairs, sems)
    mirror = mirror_matrix()
    piece_rows = piece // INNER * chan_dev
    for n in range(pieces):
        copies[n].wait()
        sides = []
        for side in range(2):
            sides.append(
                jnp.concatenate(
                    [
                        x_ref[:, pl.ds(n * piece + b * INNER + side * SIDE, SIDE)].astype(jnp.float32)
                        for b in range(piece // INNER)
                    ],
                    axis=0,
                )
            )
        before = jnp.dot(sides[0].astype(jnp.bfloat16), mirror, preferred_element_type=jnp.float32)
        rows = pl.ds(n * piece_rows, piece_rows)
        sum_ref[rows, :] = (sides[1] + before).astype(jnp.bfloat16)
        diff_ref[rows, :] = (sides[1] - before).astype(jnp.bfloat16)
    lane = lane_ids(chan_dev)

    def multiply(n):
        copies[pieces if n == 0 else pieces + 3 + n].wait()
        product_ref[n % 2, :, :CHUNK] = jnp.dot(
            sum_ref[...], table_ref[n, :, :CHUNK], preferred_element_type=jnp.float32
        )
        product_ref[n % 2, :, CHUNK:] = jnp.dot(
            diff_ref[...], table_ref[n, :, CHUNK:], preferred_element_type=jnp.float32
        )

    multiply(0)
    for copy in copies[pieces + 1 : pieces + 4]:
        copy.wait()
    for n in range(chunks):
        if n + 1 < chunks:
            multiply(n + 1)
        chunk = pl.ds(n * CHUNK, CHUNK)
        high_cos, high_sin = high_turns(high_ref[:, :, chunk], start_ref[:, chunk])
        for tile in range(CHUNK // LANES):
            cols = pl.ds(tile * LANES, LANES)
            sin_cols = pl.ds(CHUNK + tile * LANES, LANES)
            lanes = pl.ds(n * CHUNK + tile * LANES, LANES)
            low_cos = [low_ref[0, pl.ds(b, 1), lanes] for b in range(LOW)]
            low_sin = [low_ref[1, pl.ds(b, 1), lanes] for b in range(LOW)]
            real = imag = None
            for h in range(highs):
                part_real = part_imag = None
                for b in range(LOW):
                    rows = pl.ds(h * span + b * chan_dev, chan_dev)
                    by_cos = product_ref[n % 2, rows, cols]
                    by_sin = product_ref[n % 2, rows, sin_cols]
                    re = by_cos * low_cos[b] - by_sin * low_sin[b]
                    im = by_cos * low_sin[b] + by_sin * low_cos[b]
                    part_real = re if b == 0 else part_real + re
                    part_imag = im if b == 0 else part_imag + im
                cos_h = high_cos[h : h + 1, tile * LANES : (tile + 1) * LANES]
                sin_h = high_sin[h : h + 1, tile * LANES : (tile + 1) * LANES]
                re = part_real * cos_h - part_imag * sin_h
                im = part_real * sin_h + part_imag * cos_h
                real = re if h == 0 else real + re
                imag = im if h == 0 else imag + im
            imag = -imag
            owner = (n * CHUNK + tile * LANES) // HALF
            out_ref[owner] = jnp.where(lane < HALF, real, pltpu.roll(imag, HALF, 1)).astype(
                out_ref.dtype
            )
            out_ref[owner + 1] = jnp.where(lane < HALF, pltpu.roll(real, HALF, 1), imag).astype(
                out_ref.dtype
            )


def forward(where, x, table, low, high, start):
    chan_dev, time_dev = x.shape
    rows = time_dev // INNER * chan_dev
    hbm = pl.BlockSpec(memory_space=pltpu.HBM)
    return pl.pallas_call(
        forward_kernel,
        in_specs=[pl.BlockSpec(memory_space=pltpu.SMEM)] + [hbm] * 5,
        out_specs=pl.BlockSpec(memory_space=pltpu.VMEM),
        scratch_shapes=[
            pltpu.VMEM(x.shape, x.dtype),
            pltpu.VMEM(table.shape, table.dtype),
            pltpu.VMEM(low.shape, low.dtype),
            pltpu.VMEM(high.shape, high.dtype),
            pltpu.VMEM(start.shape[1:], start.dtype),
            pltpu.VMEM((rows, SIDE), jnp.bfloat16),
            pltpu.VMEM((rows, SIDE), jnp.bfloat16),
            pltpu.VMEM((2, rows, 2 * CHUNK), jnp.float32),
            pltpu.SemaphoreType.DMA((MODES // CHUNK + 4,)),
        ],
        out_shape=jax.ShapeDtypeStruct((MODES // HALF, chan_dev, LANES), jnp.bfloat16),
        cost_estimate=pl.CostEstimate(
            flops=2 * chan_dev * time_dev * MODES, bytes_accessed=4 << 20, transcendentals=0
        ),
        name="forward_modes",
    )(where, x, table, low, high, start)


def inverse_kernel(
    where_ref, mixed_ref, table_hbm, low_hbm, high_hbm, start_hbm, out_ref,
    table_ref, low_ref, high_ref, start_ref, turned_ref, even_ref, odd_ref, sems,
):
    chan_dev = mixed_ref.shape[1]
    highs = high_ref.shape[1]
    span = LOW * chan_dev
    chunks = MODES // SPAN
    pairs = [(low_hbm, low_ref), (high_hbm, high_ref), (start_hbm.at[where_ref[0]], start_ref)]
    pairs += [(table_hbm.at[n], table_ref.at[n]) for n in range(chunks)]
    copies = start_copies(pairs, sems)
    lane = lane_ids(chan_dev)
    for copy in copies[:3]:
        copy.wait()

    def turn(n):
        chunk = pl.ds(n * SPAN, SPAN)
        high_cos, high_sin = high_turns(high_ref[:, :, chunk], start_ref[:, chunk])
        for tile in range(SPAN // LANES):
            lanes = pl.ds(n * SPAN + tile * LANES, LANES)
            owner = (n * SPAN + tile * LANES) // HALF
            first = mixed_ref[owner].astype(jnp.float32)
            second = mixed_ref[owner + 1].astype(jnp.float32)
            real = jnp.where(lane < HALF, first, pltpu.roll(second, HALF, 1))
            imag = jnp.where(lane < HALF, pltpu.roll(first, HALF, 1), second)
            low_cos = [low_ref[0, pl.ds(b, 1), lanes] for b in range(LOW)]
            low_sin = [low_ref[1, pl.ds(b, 1), lanes] for b in range(LOW)]
            for h in range(highs):
                cos_h = high_cos[h : h + 1, tile * LANES : (tile + 1) * LANES]
                sin_h = high_sin[h : h + 1, tile * LANES : (tile + 1) * LANES]
                real_h = real * cos_h - imag * sin_h
                imag_h = real * sin_h + imag * cos_h
                for b in range(0, LOW, 2):
                    rows = pl.ds(h * span + b * chan_dev, 2 * chan_dev)
                    re = [real_h * low_cos[c] - imag_h * low_sin[c] for c in (b, b + 1)]
                    im = [real_h * low_sin[c] + imag_h * low_cos[c] for c in (b, b + 1)]
                    turned_ref[n % 2, rows, pl.ds(tile * LANES, LANES)] = jnp.concatenate(
                        re, axis=0
                    ).astype(jnp.bfloat16)
                    turned_ref[n % 2, rows, pl.ds(SPAN + tile * LANES, LANES)] = jnp.concatenate(
                        im, axis=0
                    ).astype(jnp.bfloat16)

    turn(0)
    for n in range(chunks):
        copies[3 + n].wait()
        even = jnp.dot(
            turned_ref[n % 2, :, :SPAN], table_ref[n, :SPAN, :], preferred_element_type=jnp.float32
        )
        odd = jnp.dot(
            turned_ref[n % 2, :, SPAN:], table_ref[n, SPAN:, :], preferred_element_type=jnp.float32
        )
        if n == 0:
            even_ref[...] = even
            odd_ref[...] = odd
        elif n + 1 < chunks:
            even_ref[...] += even
            odd_ref[...] += odd
        if n + 1 < chunks:
            turn(n + 1)
    even = even_ref[...] + even
    odd = odd_ref[...] + odd
    after = even - odd
    mirrored = even + odd
    mirror = mirror_matrix()
    upper = mirrored.astype(jnp.bfloat16)
    lower = (mirrored - upper.astype(jnp.float32)).astype(jnp.bfloat16)
    before = jnp.dot(upper, mirror, preferred_element_type=jnp.float32)
    before = before + jnp.dot(lower, mirror, preferred_element_type=jnp.float32)
    for b in range(highs * LOW):
        rows = slice(b * chan_dev, (b + 1) * chan_dev)
        out_ref[:, pl.ds(b * INNER, SIDE)] = before[rows]
        out_ref[:, pl.ds(b * INNER + SIDE, SIDE)] = after[rows]


def inverse(where, mixed, table, low, high, start, time_dev):
    owners, chan_dev, _ = mixed.shape
    rows = time_dev // INNER * chan_dev
    hbm = pl.BlockSpec(memory_space=pltpu.HBM)
    return pl.pallas_call(
        inverse_kernel,
        in_specs=[pl.BlockSpec(memory_space=pltpu.SMEM), pl.BlockSpec(memory_space=pltpu.VMEM)]
        + [hbm] * 4,
        out_specs=pl.BlockSpec(memory_space=pltpu.VMEM),
        scratch_shapes=[
            pltpu.VMEM(table.shape, table.dtype),
            pltpu.VMEM(low.shape, low.dtype),
            pltpu.VMEM(high.shape, high.dtype),
            pltpu.VMEM(start.shape[1:], start.dtype),
            pltpu.VMEM((2, rows, 2 * SPAN), jnp.bfloat16),
            pltpu.VMEM((rows, SIDE), jnp.float32),
            pltpu.VMEM((rows, SIDE), jnp.float32),
            pltpu.SemaphoreType.DMA((MODES // SPAN + 3,)),
        ],
        out_shape=jax.ShapeDtypeStruct((chan_dev, time_dev), jnp.float32),
        compiler_params=pltpu.CompilerParams(vmem_limit_bytes=VMEM_LIMIT),
        cost_estimate=pl.CostEstimate(
            flops=2 * chan_dev * time_dev * MODES, bytes_accessed=4 << 20, transcendentals=0
        ),
        name="inverse_modes",
    )(where, mixed, table, low, high, start)


def mix_kernel(where_ref, spec_ref, weight_ref, out_ref, turned_ref, mixed_ref, *, steps_all):
    turned_ref[...] = spec_ref[...].astype(jnp.float32).T
    mixed_ref[...] = jnp.zeros_like(mixed_ref)
    block_modes = weight_ref.shape[0]
    for m in range(block_modes):
        mode = where_ref[1] * block_modes + m
        re_row = turned_ref[pl.ds(mode, 1), :]
        im_row = turned_ref[pl.ds(HALF + mode, 1), :]
        both = jnp.concatenate([re_row, im_row, jnp.zeros((6, LANES), jnp.float32)], axis=0).astype(
            jnp.bfloat16
        )
        by_real = jnp.dot(both, weight_ref[m, 0], preferred_element_type=jnp.float32)
        by_imag = jnp.dot(both, weight_ref[m, 1], preferred_element_type=jnp.float32)
        scale = jnp.where(where_ref[0] * HALF + mode == 0, 1.0 / steps_all, 2.0 / steps_all)
        mixed_ref[pl.ds(mode, 1), :] = (by_real[0:1] - by_imag[1:2]) * scale
        mixed_ref[pl.ds(HALF + mode, 1), :] = (by_imag[0:1] + by_real[1:2]) * scale
    out_ref[...] = mixed_ref[...].T.astype(out_ref.dtype)


def mix(where, spec, weight, steps_all):
    return pl.pallas_call(
        lambda *refs: mix_kernel(*refs, steps_all=steps_all),
        in_specs=[
            pl.BlockSpec(memory_space=pltpu.SMEM),
            pl.BlockSpec(memory_space=pltpu.VMEM),
            pl.BlockSpec(memory_space=pltpu.VMEM),
        ],
        out_specs=pl.BlockSpec(memory_space=pltpu.VMEM),
        scratch_shapes=[pltpu.VMEM((128, LANES), jnp.float32), pltpu.VMEM((128, LANES), jnp.float32)],
        out_shape=jax.ShapeDtypeStruct(spec.shape, jnp.bfloat16),
        compiler_params=pltpu.CompilerParams(vmem_limit_bytes=4 << 20),
        name="mix_modes",
    )(where, spec, weight)


def output_kernel(weight_ref, bias_ref, spectral_ref, x_hbm, out_hbm, x_ref, out_ref, sems, out_sems):
    chan_dev, time_dev = out_ref.shape
    parts = x_ref.shape[0]
    width = time_dev // parts
    half = width // 2
    copies = start_copies(
        [(x_hbm.at[:, pl.ds(n * width, width)], x_ref.at[n]) for n in range(parts)], sems
    )
    weight = weight_ref[...].astype(jnp.float32)
    none = jnp.zeros_like(weight)
    stacked = jnp.concatenate(
        [jnp.concatenate([weight, none], axis=1), jnp.concatenate([none, weight], axis=1)], axis=0
    ).astype(jnp.bfloat16)
    row = lax.broadcasted_iota(jnp.int32, (chan_dev, 1), 0)
    bias = jnp.zeros((chan_dev, 1), jnp.float32)
    for c in range(chan_dev):
        bias = jnp.where(row == c, bias_ref[c], bias)
    results = []
    for n in range(parts):
        copies[n].wait()
        x = jnp.concatenate([x_ref[n, :, :half], x_ref[n, :, half:]], axis=0)
        skip = jnp.dot(stacked, x, preferred_element_type=jnp.float32)
        for side in range(2):
            cols = pl.ds(n * width + side * half, half)
            total = spectral_ref[:, cols] + skip[side * chan_dev : (side + 1) * chan_dev] + bias
            gelu = 0.5 * total * (1.0 + lax.erf(total * math.sqrt(0.5)))
            out_ref[:, cols] = gelu.astype(out_ref.dtype)
        cols = pl.ds(n * width, width)
        result = pltpu.make_async_copy(out_ref.at[:, cols], out_hbm.at[:, cols], out_sems.at[n])
        result.start()
        results.append(result)
    for result in results:
        result.wait()


def output(weight, bias, spectral, x):
    chan_dev, time_dev = spectral.shape
    parts = 8
    vmem = pl.BlockSpec(memory_space=pltpu.VMEM)
    hbm = pl.BlockSpec(memory_space=pltpu.HBM)
    return pl.pallas_call(
        output_kernel,
        in_specs=[vmem, pl.BlockSpec(memory_space=pltpu.SMEM), vmem, hbm],
        out_specs=hbm,
        scratch_shapes=[
            pltpu.VMEM((parts, x.shape[0], time_dev // parts), x.dtype),
            pltpu.VMEM((chan_dev, time_dev), jnp.bfloat16),
            pltpu.SemaphoreType.DMA((parts,)),
            pltpu.SemaphoreType.DMA((parts,)),
        ],
        out_shape=jax.ShapeDtypeStruct((chan_dev, time_dev), jnp.bfloat16),
        compiler_params=pltpu.CompilerParams(vmem_limit_bytes=VMEM_LIMIT),
        cost_estimate=pl.CostEstimate(
            flops=2 * 2 * chan_dev * x.shape[0] * time_dev, bytes_accessed=10 << 20, transcendentals=0
        ),
        name="skip_and_output",
    )(weight, bias, spectral, x)


def sum_and_copy(arrived, copies):
    total = jnp.sum(arrived.astype(jnp.float32), axis=0).astype(jnp.bfloat16)
    return jnp.broadcast_to(total[None], (copies, *total.shape))


def shards(records, spectral_weight, skip_weight, skip_bias):
    groups, chan_dev, time_dev = records.shape
    tm_count = lax.axis_size("tm")
    chan_count = lax.axis_size("chan")
    steps_all = time_dev * tm_count
    forward_table, inverse_table, low, high, start = tables(steps_all, time_dev)
    where = jnp.stack([lax.axis_index("tm"), lax.axis_index("chan")]).astype(jnp.int32)
    x = records.reshape(chan_dev, time_dev)

    gathered = lax.all_gather(x, "chan", axis=0, tiled=True)

    partial = forward(where, x, forward_table, low, high, start)
    arrived = lax.all_to_all(partial, "tm", 0, 0, tiled=True)
    spectrum = sum_and_copy(arrived, chan_count)
    spectrum = lax.all_to_all(spectrum, "chan", 0, 0, tiled=True)
    mixed = mix(where, spectrum.reshape(-1, LANES), spectral_weight, steps_all)
    mixed = lax.all_to_all(mixed.reshape(spectrum.shape), "chan", 0, 0, tiled=True)
    mixed = sum_and_copy(mixed, tm_count)
    mixed = lax.all_to_all(mixed, "tm", 0, 0, tiled=True)
    spectral = inverse(where, mixed, inverse_table, low, high, start, time_dev)

    out = output(skip_weight, skip_bias, spectral, gathered)
    return out.reshape(groups, chan_dev, time_dev)


def solution(mesh):
    return jax.shard_map(
        shards,
        mesh=mesh,
        in_specs=(
            P(None, "chan", "tm"),
            P(("tm", "chan"), None, None, None),
            P("chan", None),
            P("chan"),
        ),
        out_specs=P(None, "chan", "tm"),
        check_vma=False,
    )
```

```python
import math

import jax
import jax.numpy as jnp
import numpy as np
from jax import lax
from jax.experimental import pallas as pl
from jax.experimental.pallas import tpu as pltpu
from jax.sharding import PartitionSpec as P

MODES = 2048
INNER = 1024
SIDE = INNER // 2
CHUNK = 512
SPAN = 512
LOW = 8
LANES = 128
HALF = 64
VMEM_LIMIT = 52 << 20


def tables(steps_all, time_dev):
    tm_count = steps_all // time_dev
    blocks = time_dev // INNER
    modes = np.arange(MODES, dtype=np.int64)

    def turn(half_steps):
        angle = half_steps[:, None] * modes[None, :] % (2 * steps_all) * (math.pi / steps_all)
        return np.cos(angle), np.sin(angle)

    inner_cos, inner_sin = turn(2 * np.arange(SIDE, dtype=np.int64) + 1)

    def split(a, width):
        return a.reshape(SIDE, MODES // width, width).transpose(1, 0, 2)

    forward = np.concatenate([split(inner_cos, CHUNK), split(inner_sin, CHUNK)], axis=2)
    inverse = np.concatenate([split(inner_cos, SPAN), split(inner_sin, SPAN)], axis=2)
    inverse = inverse.transpose(0, 2, 1)
    low = np.stack(turn(np.arange(LOW, dtype=np.int64) * (2 * INNER) + INNER - 1))
    high = np.stack(turn(np.arange(blocks // LOW, dtype=np.int64) * (2 * INNER * LOW)))
    start = np.stack(turn(np.arange(tm_count, dtype=np.int64) * (2 * time_dev)), axis=1)
    return (
        np.ascontiguousarray(forward).astype(jnp.bfloat16),
        np.ascontiguousarray(inverse).astype(jnp.bfloat16),
        low.astype(np.float32),
        high.astype(np.float32),
        start.astype(np.float32),
    )


def lane_ids(rows):
    return lax.broadcasted_iota(jnp.int32, (rows, LANES), 1)


def mirror_matrix():
    row = lax.broadcasted_iota(jnp.int32, (SIDE, SIDE), 0)
    col = lax.broadcasted_iota(jnp.int32, (SIDE, SIDE), 1)
    return jnp.where(row + col == SIDE - 1, 1.0, 0.0).astype(jnp.bfloat16)


def start_copies(pairs, sems):
    copies = [pltpu.make_async_copy(src, dst, sems.at[n]) for n, (src, dst) in enumerate(pairs)]
    for copy in copies:
        copy.start()
    return copies


def high_turns(high, start):
    cos_s, sin_s = start[0:1], start[1:2]
    return high[0] * cos_s - high[1] * sin_s, high[0] * sin_s + high[1] * cos_s


def forward_kernel(
    x_hbm, table_hbm, low_hbm, high_hbm, start_hbm, out_ref,
    x_ref, table_ref, low_ref, high_ref, start_ref, sum_ref, diff_ref, product_ref, sems,
):
    chan_dev, time_dev = x_ref.shape
    highs = high_ref.shape[1]
    span = LOW * chan_dev
    chunks = MODES // CHUNK
    pieces = 1
    piece = time_dev // pieces
    pairs = [
        (x_hbm.at[:, pl.ds(n * piece, piece)], x_ref.at[:, pl.ds(n * piece, piece)])
        for n in range(pieces)
    ]
    pairs += [(table_hbm.at[0], table_ref.at[0])]
    pairs += [(low_hbm, low_ref), (high_hbm, high_ref), (start_hbm.at[lax.axis_index("tm")], start_ref)]
    pairs += [(table_hbm.at[n], table_ref.at[n]) for n in range(1, chunks)]
    copies = start_copies(pairs, sems)
    mirror = mirror_matrix()
    piece_rows = piece // INNER * chan_dev
    for n in range(pieces):
        copies[n].wait()
        sides = []
        for side in range(2):
            sides.append(
                jnp.concatenate(
                    [
                        x_ref[:, pl.ds(n * piece + b * INNER + side * SIDE, SIDE)].astype(jnp.float32)
                        for b in range(piece // INNER)
                    ],
                    axis=0,
                )
            )
        before = jnp.dot(sides[0].astype(jnp.bfloat16), mirror, preferred_element_type=jnp.float32)
        rows = pl.ds(n * piece_rows, piece_rows)
        sum_ref[rows, :] = (sides[1] + before).astype(jnp.bfloat16)
        diff_ref[rows, :] = (sides[1] - before).astype(jnp.bfloat16)
    lane = lane_ids(chan_dev)

    def multiply(n):
        copies[pieces if n == 0 else pieces + 3 + n].wait()
        product_ref[n % 2, :, :CHUNK] = jnp.dot(
            sum_ref[...], table_ref[n, :, :CHUNK], preferred_element_type=jnp.float32
        )
        product_ref[n % 2, :, CHUNK:] = jnp.dot(
            diff_ref[...], table_ref[n, :, CHUNK:], preferred_element_type=jnp.float32
        )

    multiply(0)
    for copy in copies[pieces + 1 : pieces + 4]:
        copy.wait()
    for n in range(chunks):
        if n + 1 < chunks:
            multiply(n + 1)
        chunk = pl.ds(n * CHUNK, CHUNK)
        high_cos, high_sin = high_turns(high_ref[:, :, chunk], start_ref[:, chunk])
        for tile in range(CHUNK // LANES):
            cols = pl.ds(tile * LANES, LANES)
            sin_cols = pl.ds(CHUNK + tile * LANES, LANES)
            lanes = pl.ds(n * CHUNK + tile * LANES, LANES)
            low_cos = [low_ref[0, pl.ds(b, 1), lanes] for b in range(LOW)]
            low_sin = [low_ref[1, pl.ds(b, 1), lanes] for b in range(LOW)]
            real = imag = None
            for h in range(highs):
                part_real = part_imag = None
                for b in range(LOW):
                    rows = pl.ds(h * span + b * chan_dev, chan_dev)
                    by_cos = product_ref[n % 2, rows, cols]
                    by_sin = product_ref[n % 2, rows, sin_cols]
                    re = by_cos * low_cos[b] - by_sin * low_sin[b]
                    im = by_cos * low_sin[b] + by_sin * low_cos[b]
                    part_real = re if b == 0 else part_real + re
                    part_imag = im if b == 0 else part_imag + im
                cos_h = high_cos[h : h + 1, tile * LANES : (tile + 1) * LANES]
                sin_h = high_sin[h : h + 1, tile * LANES : (tile + 1) * LANES]
                re = part_real * cos_h - part_imag * sin_h
                im = part_real * sin_h + part_imag * cos_h
                real = re if h == 0 else real + re
                imag = im if h == 0 else imag + im
            imag = -imag
            owner = (n * CHUNK + tile * LANES) // HALF
            out_ref[owner] = jnp.where(lane < HALF, real, pltpu.roll(imag, HALF, 1)).astype(
                out_ref.dtype
            )
            out_ref[owner + 1] = jnp.where(lane < HALF, pltpu.roll(real, HALF, 1), imag).astype(
                out_ref.dtype
            )


def forward(x, table, low, high, start):
    chan_dev, time_dev = x.shape
    rows = time_dev // INNER * chan_dev
    hbm = pl.BlockSpec(memory_space=pltpu.HBM)
    return pl.pallas_call(
        forward_kernel,
        in_specs=[hbm] * 5,
        out_specs=pl.BlockSpec(memory_space=pltpu.VMEM),
        scratch_shapes=[
            pltpu.VMEM(x.shape, x.dtype),
            pltpu.VMEM(table.shape, table.dtype),
            pltpu.VMEM(low.shape, low.dtype),
            pltpu.VMEM(high.shape, high.dtype),
            pltpu.VMEM(start.shape[1:], start.dtype),
            pltpu.VMEM((rows, SIDE), jnp.bfloat16),
            pltpu.VMEM((rows, SIDE), jnp.bfloat16),
            pltpu.VMEM((2, rows, 2 * CHUNK), jnp.float32),
            pltpu.SemaphoreType.DMA((MODES // CHUNK + 4,)),
        ],
        out_shape=jax.ShapeDtypeStruct((MODES // HALF, chan_dev, LANES), jnp.bfloat16),
        cost_estimate=pl.CostEstimate(
            flops=2 * chan_dev * time_dev * MODES, bytes_accessed=4 << 20, transcendentals=0
        ),
        name="forward_modes",
    )(x, table, low, high, start)


def inverse_kernel(
    mixed_ref, table_hbm, low_hbm, high_hbm, start_hbm, out_ref,
    table_ref, low_ref, high_ref, start_ref, turned_ref, even_ref, odd_ref, sems,
):
    chan_dev = mixed_ref.shape[1]
    highs = high_ref.shape[1]
    span = LOW * chan_dev
    chunks = MODES // SPAN
    pairs = [(low_hbm, low_ref), (high_hbm, high_ref), (start_hbm.at[lax.axis_index("tm")], start_ref)]
    pairs += [(table_hbm.at[n], table_ref.at[n]) for n in range(chunks)]
    copies = start_copies(pairs, sems)
    lane = lane_ids(chan_dev)
    for copy in copies[:3]:
        copy.wait()

    def turn(n):
        chunk = pl.ds(n * SPAN, SPAN)
        high_cos, high_sin = high_turns(high_ref[:, :, chunk], start_ref[:, chunk])
        for tile in range(SPAN // LANES):
            lanes = pl.ds(n * SPAN + tile * LANES, LANES)
            owner = (n * SPAN + tile * LANES) // HALF
            first = mixed_ref[owner].astype(jnp.float32)
            second = mixed_ref[owner + 1].astype(jnp.float32)
            real = jnp.where(lane < HALF, first, pltpu.roll(second, HALF, 1))
            imag = jnp.where(lane < HALF, pltpu.roll(first, HALF, 1), second)
            low_cos = [low_ref[0, pl.ds(b, 1), lanes] for b in range(LOW)]
            low_sin = [low_ref[1, pl.ds(b, 1), lanes] for b in range(LOW)]
            for h in range(highs):
                cos_h = high_cos[h : h + 1, tile * LANES : (tile + 1) * LANES]
                sin_h = high_sin[h : h + 1, tile * LANES : (tile + 1) * LANES]
                real_h = real * cos_h - imag * sin_h
                imag_h = real * sin_h + imag * cos_h
                for b in range(0, LOW, 2):
                    rows = pl.ds(h * span + b * chan_dev, 2 * chan_dev)
                    re = [real_h * low_cos[c] - imag_h * low_sin[c] for c in (b, b + 1)]
                    im = [real_h * low_sin[c] + imag_h * low_cos[c] for c in (b, b + 1)]
                    turned_ref[n % 2, rows, pl.ds(tile * LANES, LANES)] = jnp.concatenate(
                        re, axis=0
                    ).astype(jnp.bfloat16)
                    turned_ref[n % 2, rows, pl.ds(SPAN + tile * LANES, LANES)] = jnp.concatenate(
                        im, axis=0
                    ).astype(jnp.bfloat16)

    turn(0)
    for n in range(chunks):
        copies[3 + n].wait()
        even = jnp.dot(
            turned_ref[n % 2, :, :SPAN], table_ref[n, :SPAN, :], preferred_element_type=jnp.float32
        )
        odd = jnp.dot(
            turned_ref[n % 2, :, SPAN:], table_ref[n, SPAN:, :], preferred_element_type=jnp.float32
        )
        if n == 0:
            even_ref[...] = even
            odd_ref[...] = odd
        elif n + 1 < chunks:
            even_ref[...] += even
            odd_ref[...] += odd
        if n + 1 < chunks:
            turn(n + 1)
    even = even_ref[...] + even
    odd = odd_ref[...] + odd
    after = even - odd
    mirrored = even + odd
    mirror = mirror_matrix()
    upper = mirrored.astype(jnp.bfloat16)
    lower = (mirrored - upper.astype(jnp.float32)).astype(jnp.bfloat16)
    before = jnp.dot(upper, mirror, preferred_element_type=jnp.float32)
    before = before + jnp.dot(lower, mirror, preferred_element_type=jnp.float32)
    for b in range(highs * LOW):
        rows = slice(b * chan_dev, (b + 1) * chan_dev)
        out_ref[:, pl.ds(b * INNER, SIDE)] = before[rows]
        out_ref[:, pl.ds(b * INNER + SIDE, SIDE)] = after[rows]


def inverse(mixed, table, low, high, start, time_dev):
    owners, chan_dev, _ = mixed.shape
    rows = time_dev // INNER * chan_dev
    hbm = pl.BlockSpec(memory_space=pltpu.HBM)
    return pl.pallas_call(
        inverse_kernel,
        in_specs=[pl.BlockSpec(memory_space=pltpu.VMEM)] + [hbm] * 4,
        out_specs=pl.BlockSpec(memory_space=pltpu.VMEM),
        scratch_shapes=[
            pltpu.VMEM(table.shape, table.dtype),
            pltpu.VMEM(low.shape, low.dtype),
            pltpu.VMEM(high.shape, high.dtype),
            pltpu.VMEM(start.shape[1:], start.dtype),
            pltpu.VMEM((2, rows, 2 * SPAN), jnp.bfloat16),
            pltpu.VMEM((rows, SIDE), jnp.float32),
            pltpu.VMEM((rows, SIDE), jnp.float32),
            pltpu.SemaphoreType.DMA((MODES // SPAN + 3,)),
        ],
        out_shape=jax.ShapeDtypeStruct((chan_dev, time_dev), jnp.float32),
        compiler_params=pltpu.CompilerParams(vmem_limit_bytes=VMEM_LIMIT),
        cost_estimate=pl.CostEstimate(
            flops=2 * chan_dev * time_dev * MODES, bytes_accessed=4 << 20, transcendentals=0
        ),
        name="inverse_modes",
    )(mixed, table, low, high, start)


def mix_kernel(spec_ref, weight_ref, out_ref, turned_ref, mixed_ref, *, steps_all):
    time_index = lax.axis_index("tm")
    chan_index = lax.axis_index("chan")
    turned_ref[...] = spec_ref[...].astype(jnp.float32).T
    mixed_ref[...] = jnp.zeros_like(mixed_ref)
    block_modes = weight_ref.shape[0]
    for m in range(block_modes):
        mode = chan_index * block_modes + m
        re_row = turned_ref[pl.ds(mode, 1), :]
        im_row = turned_ref[pl.ds(HALF + mode, 1), :]
        both = jnp.concatenate([re_row, im_row, jnp.zeros((6, LANES), jnp.float32)], axis=0).astype(
            jnp.bfloat16
        )
        by_real = jnp.dot(both, weight_ref[m, 0], preferred_element_type=jnp.float32)
        by_imag = jnp.dot(both, weight_ref[m, 1], preferred_element_type=jnp.float32)
        scale = jnp.where(time_index * HALF + mode == 0, 1.0 / steps_all, 2.0 / steps_all)
        mixed_ref[pl.ds(mode, 1), :] = (by_real[0:1] - by_imag[1:2]) * scale
        mixed_ref[pl.ds(HALF + mode, 1), :] = (by_imag[0:1] + by_real[1:2]) * scale
    out_ref[...] = mixed_ref[...].T.astype(out_ref.dtype)


def mix(spec, weight, steps_all):
    return pl.pallas_call(
        lambda *refs: mix_kernel(*refs, steps_all=steps_all),
        in_specs=[pl.BlockSpec(memory_space=pltpu.VMEM)] * 2,
        out_specs=pl.BlockSpec(memory_space=pltpu.VMEM),
        scratch_shapes=[pltpu.VMEM((128, LANES), jnp.float32), pltpu.VMEM((128, LANES), jnp.float32)],
        out_shape=jax.ShapeDtypeStruct(spec.shape, jnp.bfloat16),
        compiler_params=pltpu.CompilerParams(vmem_limit_bytes=4 << 20),
        name="mix_modes",
    )(spec, weight)


def output_kernel(weight_ref, bias_ref, spectral_ref, x_hbm, out_hbm, x_ref, out_ref, sems, out_sems):
    chan_dev, time_dev = out_ref.shape
    parts = x_ref.shape[0]
    width = time_dev // parts
    half = width // 2
    copies = start_copies(
        [(x_hbm.at[:, pl.ds(n * width, width)], x_ref.at[n]) for n in range(parts)], sems
    )
    weight = weight_ref[...].astype(jnp.float32)
    none = jnp.zeros_like(weight)
    stacked = jnp.concatenate(
        [jnp.concatenate([weight, none], axis=1), jnp.concatenate([none, weight], axis=1)], axis=0
    ).astype(jnp.bfloat16)
    row = lax.broadcasted_iota(jnp.int32, (chan_dev, 1), 0)
    bias = jnp.zeros((chan_dev, 1), jnp.float32)
    for c in range(chan_dev):
        bias = jnp.where(row == c, bias_ref[c], bias)
    results = []
    for n in range(parts):
        copies[n].wait()
        x = jnp.concatenate([x_ref[n, :, :half], x_ref[n, :, half:]], axis=0)
        skip = jnp.dot(stacked, x, preferred_element_type=jnp.float32)
        for side in range(2):
            cols = pl.ds(n * width + side * half, half)
            total = spectral_ref[:, cols] + skip[side * chan_dev : (side + 1) * chan_dev] + bias
            gelu = 0.5 * total * (1.0 + lax.erf(total * math.sqrt(0.5)))
            out_ref[:, cols] = gelu.astype(out_ref.dtype)
        cols = pl.ds(n * width, width)
        result = pltpu.make_async_copy(out_ref.at[:, cols], out_hbm.at[:, cols], out_sems.at[n])
        result.start()
        results.append(result)
    for result in results:
        result.wait()


def output(weight, bias, spectral, x):
    chan_dev, time_dev = spectral.shape
    parts = 8
    vmem = pl.BlockSpec(memory_space=pltpu.VMEM)
    hbm = pl.BlockSpec(memory_space=pltpu.HBM)
    return pl.pallas_call(
        output_kernel,
        in_specs=[vmem, pl.BlockSpec(memory_space=pltpu.SMEM), vmem, hbm],
        out_specs=hbm,
        scratch_shapes=[
            pltpu.VMEM((parts, x.shape[0], time_dev // parts), x.dtype),
            pltpu.VMEM((chan_dev, time_dev), jnp.bfloat16),
            pltpu.SemaphoreType.DMA((parts,)),
            pltpu.SemaphoreType.DMA((parts,)),
        ],
        out_shape=jax.ShapeDtypeStruct((chan_dev, time_dev), jnp.bfloat16),
        compiler_params=pltpu.CompilerParams(vmem_limit_bytes=VMEM_LIMIT),
        cost_estimate=pl.CostEstimate(
            flops=2 * 2 * chan_dev * x.shape[0] * time_dev, bytes_accessed=10 << 20, transcendentals=0
        ),
        name="skip_and_output",
    )(weight, bias, spectral, x)


def sum_and_copy(arrived, copies):
    total = jnp.sum(arrived.astype(jnp.float32), axis=0).astype(jnp.bfloat16)
    return jnp.broadcast_to(total[None], (copies, *total.shape))


def shards(records, spectral_weight, skip_weight, skip_bias):
    groups, chan_dev, time_dev = records.shape
    tm_count = lax.axis_size("tm")
    chan_count = lax.axis_size("chan")
    steps_all = time_dev * tm_count
    forward_table, inverse_table, low, high, start = tables(steps_all, time_dev)
    x = records.reshape(chan_dev, time_dev)

    gathered = lax.all_gather(x, "chan", axis=0, tiled=True)

    partial = forward(x, forward_table, low, high, start)
    arrived = lax.all_to_all(partial, "tm", 0, 0, tiled=True)
    spectrum = sum_and_copy(arrived, chan_count)
    spectrum = lax.all_to_all(spectrum, "chan", 0, 0, tiled=True)
    mixed = mix(spectrum.reshape(-1, LANES), spectral_weight, steps_all)
    mixed = lax.all_to_all(mixed.reshape(spectrum.shape), "chan", 0, 0, tiled=True)
    mixed = sum_and_copy(mixed, tm_count)
    mixed = lax.all_to_all(mixed, "tm", 0, 0, tiled=True)
    spectral = inverse(mixed, inverse_table, low, high, start, time_dev)

    out = output(skip_weight, skip_bias, spectral, gathered)
    return out.reshape(groups, chan_dev, time_dev)


def solution(mesh):
    return jax.shard_map(
        shards,
        mesh=mesh,
        in_specs=(
            P(None, "chan", "tm"),
            P(("tm", "chan"), None, None, None),
            P("chan", None),
            P("chan"),
        ),
        out_specs=P(None, "chan", "tm"),
        check_vma=False,
    )
```

```python
import math

import jax
import jax.numpy as jnp
import numpy as np
from jax import lax
from jax.experimental import pallas as pl
from jax.experimental.pallas import tpu as pltpu
from jax.sharding import PartitionSpec as P

MODES = 2048
INNER = 1024
SIDE = INNER // 2
MIRROR = 256
CHUNK = 512
SPAN = 512
LOW = 16
LANES = 128
HALF = 64
VMEM_LIMIT = 52 << 20


def tables(steps_all, time_dev):
    tm_count = steps_all // time_dev
    blocks = time_dev // INNER
    modes = np.arange(MODES, dtype=np.int64)

    def turn(half_steps):
        angle = half_steps[:, None] * modes[None, :] % (2 * steps_all) * (math.pi / steps_all)
        return np.cos(angle), np.sin(angle)

    inner_cos, inner_sin = turn(2 * np.arange(SIDE, dtype=np.int64) + 1)

    def split(a, width):
        return a.reshape(SIDE, MODES // width, width).transpose(1, 0, 2)

    forward = np.concatenate([split(inner_cos, CHUNK), split(inner_sin, CHUNK)], axis=2)
    inverse = np.concatenate([split(inner_cos, SPAN), split(inner_sin, SPAN)], axis=2)
    inverse = inverse.transpose(0, 2, 1)
    low = np.stack(turn(np.arange(LOW, dtype=np.int64) * (2 * INNER) + INNER - 1))
    high = np.stack(turn(np.arange(blocks // LOW, dtype=np.int64) * (2 * INNER * LOW)))
    start = np.stack(turn(np.arange(tm_count, dtype=np.int64) * (2 * time_dev)), axis=1)
    return (
        np.ascontiguousarray(forward).astype(jnp.bfloat16),
        np.ascontiguousarray(inverse).astype(jnp.bfloat16),
        low.astype(np.float32),
        high.astype(np.float32),
        start.astype(np.float32),
    )


def lane_ids(rows):
    return lax.broadcasted_iota(jnp.int32, (rows, LANES), 1)


def mirror_matrix():
    row = lax.broadcasted_iota(jnp.int32, (MIRROR, MIRROR), 0)
    col = lax.broadcasted_iota(jnp.int32, (MIRROR, MIRROR), 1)
    return jnp.where(row + col == MIRROR - 1, 1.0, 0.0).astype(jnp.bfloat16)


def start_copies(pairs, sems):
    copies = [pltpu.make_async_copy(src, dst, sems.at[n]) for n, (src, dst) in enumerate(pairs)]
    for copy in copies:
        copy.start()
    return copies


def high_turns(high, start):
    cos_s, sin_s = start[0:1], start[1:2]
    return high[0] * cos_s - high[1] * sin_s, high[0] * sin_s + high[1] * cos_s


def forward_kernel(
    x_hbm, table_hbm, low_hbm, high_hbm, start_hbm, out_ref,
    x_ref, table_ref, low_ref, high_ref, start_ref, sum_ref, diff_ref, product_ref, sems,
):
    chan_dev, time_dev = x_ref.shape
    highs = high_ref.shape[1]
    span = LOW * chan_dev
    chunks = MODES // CHUNK
    pieces = 1
    piece = time_dev // pieces
    pairs = [
        (x_hbm.at[:, pl.ds(n * piece, piece)], x_ref.at[:, pl.ds(n * piece, piece)])
        for n in range(pieces)
    ]
    pairs += [(table_hbm.at[0], table_ref.at[0])]
    pairs += [(low_hbm, low_ref), (high_hbm, high_ref), (start_hbm.at[lax.axis_index("tm")], start_ref)]
    pairs += [(table_hbm.at[n], table_ref.at[n]) for n in range(1, chunks)]
    copies = start_copies(pairs, sems)
    mirror = mirror_matrix()
    piece_rows = piece // INNER * chan_dev
    for n in range(pieces):
        copies[n].wait()
        sides = []
        for side in range(2):
            sides.append(
                jnp.concatenate(
                    [
                        x_ref[:, pl.ds(n * piece + b * INNER + side * SIDE, SIDE)].astype(jnp.float32)
                        for b in range(piece // INNER)
                    ],
                    axis=0,
                )
            )
        first = sides[0].astype(jnp.bfloat16)
        before = jnp.concatenate(
            [
                jnp.dot(
                    first[:, m * MIRROR : (m + 1) * MIRROR],
                    mirror,
                    preferred_element_type=jnp.float32,
                )
                for m in reversed(range(SIDE // MIRROR))
            ],
            axis=1,
        )
        rows = pl.ds(n * piece_rows, piece_rows)
        sum_ref[rows, :] = (sides[1] + before).astype(jnp.bfloat16)
        diff_ref[rows, :] = (sides[1] - before).astype(jnp.bfloat16)
    lane = lane_ids(chan_dev)

    def multiply(n):
        copies[pieces if n == 0 else pieces + 3 + n].wait()
        product_ref[n % 2, :, :CHUNK] = jnp.dot(
            sum_ref[...], table_ref[n, :, :CHUNK], preferred_element_type=jnp.float32
        )
        product_ref[n % 2, :, CHUNK:] = jnp.dot(
            diff_ref[...], table_ref[n, :, CHUNK:], preferred_element_type=jnp.float32
        )

    multiply(0)
    for copy in copies[pieces + 1 : pieces + 4]:
        copy.wait()
    for n in range(chunks):
        if n + 1 < chunks:
            multiply(n + 1)
        chunk = pl.ds(n * CHUNK, CHUNK)
        high_cos, high_sin = high_turns(high_ref[:, :, chunk], start_ref[:, chunk])
        for tile in range(CHUNK // LANES):
            cols = pl.ds(tile * LANES, LANES)
            sin_cols = pl.ds(CHUNK + tile * LANES, LANES)
            lanes = pl.ds(n * CHUNK + tile * LANES, LANES)
            low_cos = [low_ref[0, pl.ds(b, 1), lanes] for b in range(LOW)]
            low_sin = [low_ref[1, pl.ds(b, 1), lanes] for b in range(LOW)]
            real = imag = None
            for h in range(highs):
                part_real = part_imag = None
                for b in range(LOW):
                    rows = pl.ds(h * span + b * chan_dev, chan_dev)
                    by_cos = product_ref[n % 2, rows, cols]
                    by_sin = product_ref[n % 2, rows, sin_cols]
                    re = by_cos * low_cos[b] - by_sin * low_sin[b]
                    im = by_cos * low_sin[b] + by_sin * low_cos[b]
                    part_real = re if b == 0 else part_real + re
                    part_imag = im if b == 0 else part_imag + im
                cos_h = high_cos[h : h + 1, tile * LANES : (tile + 1) * LANES]
                sin_h = high_sin[h : h + 1, tile * LANES : (tile + 1) * LANES]
                re = part_real * cos_h - part_imag * sin_h
                im = part_real * sin_h + part_imag * cos_h
                real = re if h == 0 else real + re
                imag = im if h == 0 else imag + im
            imag = -imag
            owner = (n * CHUNK + tile * LANES) // HALF
            out_ref[owner] = jnp.where(lane < HALF, real, pltpu.roll(imag, HALF, 1)).astype(
                out_ref.dtype
            )
            out_ref[owner + 1] = jnp.where(lane < HALF, pltpu.roll(real, HALF, 1), imag).astype(
                out_ref.dtype
            )


def forward(x, table, low, high, start):
    chan_dev, time_dev = x.shape
    rows = time_dev // INNER * chan_dev
    hbm = pl.BlockSpec(memory_space=pltpu.HBM)
    return pl.pallas_call(
        forward_kernel,
        in_specs=[hbm] * 5,
        out_specs=pl.BlockSpec(memory_space=pltpu.VMEM),
        scratch_shapes=[
            pltpu.VMEM(x.shape, x.dtype),
            pltpu.VMEM(table.shape, table.dtype),
            pltpu.VMEM(low.shape, low.dtype),
            pltpu.VMEM(high.shape, high.dtype),
            pltpu.VMEM(start.shape[1:], start.dtype),
            pltpu.VMEM((rows, SIDE), jnp.bfloat16),
            pltpu.VMEM((rows, SIDE), jnp.bfloat16),
            pltpu.VMEM((2, rows, 2 * CHUNK), jnp.float32),
            pltpu.SemaphoreType.DMA((MODES // CHUNK + 4,)),
        ],
        out_shape=jax.ShapeDtypeStruct((MODES // HALF, chan_dev, LANES), jnp.bfloat16),
        cost_estimate=pl.CostEstimate(
            flops=2 * chan_dev * time_dev * MODES, bytes_accessed=4 << 20, transcendentals=0
        ),
        name="forward_modes",
    )(x, table, low, high, start)


def inverse_kernel(
    mixed_ref, table_hbm, low_hbm, high_hbm, start_hbm, out_ref,
    table_ref, low_ref, high_ref, start_ref, turned_ref, even_ref, odd_ref, sems,
):
    chan_dev = mixed_ref.shape[1]
    highs = high_ref.shape[1]
    span = LOW * chan_dev
    chunks = MODES // SPAN
    pairs = [(low_hbm, low_ref), (high_hbm, high_ref), (start_hbm.at[lax.axis_index("tm")], start_ref)]
    pairs += [(table_hbm.at[n], table_ref.at[n]) for n in range(chunks)]
    copies = start_copies(pairs, sems)
    lane = lane_ids(chan_dev)
    for copy in copies[:3]:
        copy.wait()

    def turn(n):
        chunk = pl.ds(n * SPAN, SPAN)
        high_cos, high_sin = high_turns(high_ref[:, :, chunk], start_ref[:, chunk])
        for tile in range(SPAN // LANES):
            lanes = pl.ds(n * SPAN + tile * LANES, LANES)
            owner = (n * SPAN + tile * LANES) // HALF
            first = mixed_ref[owner].astype(jnp.float32)
            second = mixed_ref[owner + 1].astype(jnp.float32)
            real = jnp.where(lane < HALF, first, pltpu.roll(second, HALF, 1))
            imag = jnp.where(lane < HALF, pltpu.roll(first, HALF, 1), second)
            low_cos = [low_ref[0, pl.ds(b, 1), lanes] for b in range(LOW)]
            low_sin = [low_ref[1, pl.ds(b, 1), lanes] for b in range(LOW)]
            for h in range(highs):
                cos_h = high_cos[h : h + 1, tile * LANES : (tile + 1) * LANES]
                sin_h = high_sin[h : h + 1, tile * LANES : (tile + 1) * LANES]
                real_h = real * cos_h - imag * sin_h
                imag_h = real * sin_h + imag * cos_h
                for b in range(0, LOW, 2):
                    rows = pl.ds(h * span + b * chan_dev, 2 * chan_dev)
                    re = [real_h * low_cos[c] - imag_h * low_sin[c] for c in (b, b + 1)]
                    im = [real_h * low_sin[c] + imag_h * low_cos[c] for c in (b, b + 1)]
                    turned_ref[n % 2, rows, pl.ds(tile * LANES, LANES)] = jnp.concatenate(
                        re, axis=0
                    ).astype(jnp.bfloat16)
                    turned_ref[n % 2, rows, pl.ds(SPAN + tile * LANES, LANES)] = jnp.concatenate(
                        im, axis=0
                    ).astype(jnp.bfloat16)

    turn(0)
    for n in range(chunks):
        copies[3 + n].wait()
        even = jnp.dot(
            turned_ref[n % 2, :, :SPAN], table_ref[n, :SPAN, :], preferred_element_type=jnp.float32
        )
        odd = jnp.dot(
            turned_ref[n % 2, :, SPAN:], table_ref[n, SPAN:, :], preferred_element_type=jnp.float32
        )
        if n == 0:
            even_ref[...] = even
            odd_ref[...] = odd
        elif n + 1 < chunks:
            even_ref[...] += even
            odd_ref[...] += odd
        if n + 1 < chunks:
            turn(n + 1)
    even = even_ref[...] + even
    odd = odd_ref[...] + odd
    after = even - odd
    mirrored = even + odd
    mirror = mirror_matrix()
    upper = mirrored.astype(jnp.bfloat16)
    lower = (mirrored - upper.astype(jnp.float32)).astype(jnp.bfloat16)
    pieces = []
    for n in reversed(range(SIDE // MIRROR)):
        cols = slice(n * MIRROR, (n + 1) * MIRROR)
        piece = jnp.dot(upper[:, cols], mirror, preferred_element_type=jnp.float32)
        pieces.append(piece + jnp.dot(lower[:, cols], mirror, preferred_element_type=jnp.float32))
    before = jnp.concatenate(pieces, axis=1)
    for b in range(highs * LOW):
        rows = slice(b * chan_dev, (b + 1) * chan_dev)
        out_ref[:, pl.ds(b * INNER, SIDE)] = before[rows]
        out_ref[:, pl.ds(b * INNER + SIDE, SIDE)] = after[rows]


def inverse(mixed, table, low, high, start, time_dev):
    owners, chan_dev, _ = mixed.shape
    rows = time_dev // INNER * chan_dev
    hbm = pl.BlockSpec(memory_space=pltpu.HBM)
    return pl.pallas_call(
        inverse_kernel,
        in_specs=[pl.BlockSpec(memory_space=pltpu.VMEM)] + [hbm] * 4,
        out_specs=pl.BlockSpec(memory_space=pltpu.VMEM),
        scratch_shapes=[
            pltpu.VMEM(table.shape, table.dtype),
            pltpu.VMEM(low.shape, low.dtype),
            pltpu.VMEM(high.shape, high.dtype),
            pltpu.VMEM(start.shape[1:], start.dtype),
            pltpu.VMEM((2, rows, 2 * SPAN), jnp.bfloat16),
            pltpu.VMEM((rows, SIDE), jnp.float32),
            pltpu.VMEM((rows, SIDE), jnp.float32),
            pltpu.SemaphoreType.DMA((MODES // SPAN + 3,)),
        ],
        out_shape=jax.ShapeDtypeStruct((chan_dev, time_dev), jnp.float32),
        compiler_params=pltpu.CompilerParams(vmem_limit_bytes=VMEM_LIMIT),
        cost_estimate=pl.CostEstimate(
            flops=2 * chan_dev * time_dev * MODES, bytes_accessed=4 << 20, transcendentals=0
        ),
        name="inverse_modes",
    )(mixed, table, low, high, start)


def mix_kernel(spec_ref, weight_ref, out_ref, turned_ref, mixed_ref, *, steps_all):
    time_index = lax.axis_index("tm")
    chan_index = lax.axis_index("chan")
    turned_ref[...] = spec_ref[...].astype(jnp.float32).T
    mixed_ref[...] = jnp.zeros_like(mixed_ref)
    block_modes = weight_ref.shape[0]
    for m in range(block_modes):
        mode = chan_index * block_modes + m
        re_row = turned_ref[pl.ds(mode, 1), :]
        im_row = turned_ref[pl.ds(HALF + mode, 1), :]
        both = jnp.concatenate([re_row, im_row, jnp.zeros((6, LANES), jnp.float32)], axis=0).astype(
            jnp.bfloat16
        )
        by_real = jnp.dot(both, weight_ref[m, 0], preferred_element_type=jnp.float32)
        by_imag = jnp.dot(both, weight_ref[m, 1], preferred_element_type=jnp.float32)
        scale = jnp.where(time_index * HALF + mode == 0, 1.0 / steps_all, 2.0 / steps_all)
        mixed_ref[pl.ds(mode, 1), :] = (by_real[0:1] - by_imag[1:2]) * scale
        mixed_ref[pl.ds(HALF + mode, 1), :] = (by_imag[0:1] + by_real[1:2]) * scale
    out_ref[...] = mixed_ref[...].T.astype(out_ref.dtype)


def mix(spec, weight, steps_all):
    return pl.pallas_call(
        lambda *refs: mix_kernel(*refs, steps_all=steps_all),
        in_specs=[pl.BlockSpec(memory_space=pltpu.VMEM)] * 2,
        out_specs=pl.BlockSpec(memory_space=pltpu.VMEM),
        scratch_shapes=[pltpu.VMEM((128, LANES), jnp.float32), pltpu.VMEM((128, LANES), jnp.float32)],
        out_shape=jax.ShapeDtypeStruct(spec.shape, jnp.bfloat16),
        compiler_params=pltpu.CompilerParams(vmem_limit_bytes=4 << 20),
        name="mix_modes",
    )(spec, weight)


def output_kernel(weight_ref, bias_ref, spectral_ref, x_hbm, out_hbm, x_ref, out_ref, sems, out_sems):
    chan_dev, time_dev = out_ref.shape
    parts = x_ref.shape[0]
    width = time_dev // parts
    half = width // 2
    copies = start_copies(
        [(x_hbm.at[:, pl.ds(n * width, width)], x_ref.at[n]) for n in range(parts)], sems
    )
    weight = weight_ref[...].astype(jnp.float32)
    none = jnp.zeros_like(weight)
    stacked = jnp.concatenate(
        [jnp.concatenate([weight, none], axis=1), jnp.concatenate([none, weight], axis=1)], axis=0
    ).astype(jnp.bfloat16)
    diagonal = lax.broadcasted_iota(jnp.int32, (chan_dev, chan_dev), 0) == lax.broadcasted_iota(
        jnp.int32, (chan_dev, chan_dev), 1
    )
    bias = jnp.sum(jnp.where(diagonal, bias_ref[...], 0.0), axis=1, keepdims=True)
    results = []
    for n in range(parts):
        copies[n].wait()
        x = jnp.concatenate([x_ref[n, :, :half], x_ref[n, :, half:]], axis=0)
        skip = jnp.dot(stacked, x, preferred_element_type=jnp.float32)
        for side in range(2):
            cols = pl.ds(n * width + side * half, half)
            total = spectral_ref[:, cols] + skip[side * chan_dev : (side + 1) * chan_dev] + bias
            gelu = 0.5 * total * (1.0 + lax.erf(total * math.sqrt(0.5)))
            out_ref[:, cols] = gelu.astype(out_ref.dtype)
        cols = pl.ds(n * width, width)
        result = pltpu.make_async_copy(out_ref.at[:, cols], out_hbm.at[:, cols], out_sems.at[n])
        result.start()
        results.append(result)
    for result in results:
        result.wait()


def output(weight, bias, spectral, x):
    chan_dev, time_dev = spectral.shape
    parts = 8
    vmem = pl.BlockSpec(memory_space=pltpu.VMEM)
    hbm = pl.BlockSpec(memory_space=pltpu.HBM)
    return pl.pallas_call(
        output_kernel,
        in_specs=[vmem, vmem, vmem, hbm],
        out_specs=hbm,
        scratch_shapes=[
            pltpu.VMEM((parts, x.shape[0], time_dev // parts), x.dtype),
            pltpu.VMEM((chan_dev, time_dev), jnp.bfloat16),
            pltpu.SemaphoreType.DMA((parts,)),
            pltpu.SemaphoreType.DMA((parts,)),
        ],
        out_shape=jax.ShapeDtypeStruct((chan_dev, time_dev), jnp.bfloat16),
        compiler_params=pltpu.CompilerParams(vmem_limit_bytes=VMEM_LIMIT),
        cost_estimate=pl.CostEstimate(
            flops=2 * 2 * chan_dev * x.shape[0] * time_dev, bytes_accessed=10 << 20, transcendentals=0
        ),
        name="skip_and_output",
    )(weight, bias, spectral, x)


def sum_and_copy(arrived, copies):
    total = jnp.sum(arrived.astype(jnp.float32), axis=0).astype(jnp.bfloat16)
    return jnp.broadcast_to(total[None], (copies, *total.shape))


def shards(records, spectral_weight, skip_weight, skip_bias):
    groups, chan_dev, time_dev = records.shape
    tm_count = lax.axis_size("tm")
    chan_count = lax.axis_size("chan")
    steps_all = time_dev * tm_count
    forward_table, inverse_table, low, high, start = tables(steps_all, time_dev)
    x = records.reshape(chan_dev, time_dev)

    gathered = lax.all_gather(x, "chan", axis=0, tiled=True)

    partial = forward(x, forward_table, low, high, start)
    arrived = lax.all_to_all(partial, "tm", 0, 0, tiled=True)
    spectrum = sum_and_copy(arrived, chan_count)
    spectrum = lax.all_to_all(spectrum, "chan", 0, 0, tiled=True)
    mixed = mix(spectrum.reshape(-1, LANES), spectral_weight, steps_all)
    mixed = lax.all_to_all(mixed.reshape(spectrum.shape), "chan", 0, 0, tiled=True)
    mixed = sum_and_copy(mixed, tm_count)
    mixed = lax.all_to_all(mixed, "tm", 0, 0, tiled=True)
    spectral = inverse(mixed, inverse_table, low, high, start, time_dev)

    out = output(skip_weight, skip_bias[None, :], spectral, gathered)
    return out.reshape(groups, chan_dev, time_dev)


def solution(mesh):
    return jax.shard_map(
        shards,
        mesh=mesh,
        in_specs=(
            P(None, "chan", "tm"),
            P(("tm", "chan"), None, None, None),
            P("chan", None),
            P("chan"),
        ),
        out_specs=P(None, "chan", "tm"),
        check_vma=False,
    )
```

```python
import math

import jax
import jax.numpy as jnp
import numpy as np
from jax import lax
from jax.experimental import pallas as pl
from jax.experimental.pallas import tpu as pltpu
from jax.sharding import PartitionSpec as P

MODES = 2048
INNER = 2048
SIDE = INNER // 2
MIRROR = 256
BAND = MODES // 2
CHUNK = 256
LOW = 16
LANES = 128
HALF = 64
VMEM_LIMIT = 52 << 20


def tables(steps_all, time_dev):
    tm_count = steps_all // time_dev
    blocks = time_dev // INNER
    pair = np.arange(BAND, dtype=np.int64)
    modes = np.concatenate([BAND + pair, BAND - 1 - pair])
    inner = 2 * np.arange(SIDE, dtype=np.int64) + 1

    def turn(half_steps, half_modes):
        angle = half_steps[:, None] * half_modes[None, :] % (4 * steps_all)
        return np.cos(angle * (math.pi / (2 * steps_all))), np.sin(angle * (math.pi / (2 * steps_all)))

    inner_cos, inner_sin = turn(inner, 2 * pair + 1)
    split = lambda a: a.reshape(SIDE, BAND // CHUNK, CHUNK).transpose(1, 0, 2)
    forward = np.concatenate([split(inner_cos), split(inner_sin)], axis=2)
    carrier = np.stack(turn(inner, np.array([2 * BAND - 1])))[:, :, 0]
    low = np.stack(turn(np.arange(LOW, dtype=np.int64) * (2 * INNER) + INNER - 1, 2 * modes))
    high = np.stack(turn(np.arange(blocks // LOW, dtype=np.int64) * (2 * INNER * LOW), 2 * modes))
    start = np.stack(turn(np.arange(tm_count, dtype=np.int64) * (2 * time_dev), 2 * modes), axis=1)
    return (
        np.ascontiguousarray(forward).astype(jnp.bfloat16),
        np.ascontiguousarray(forward.transpose(0, 2, 1)).astype(jnp.bfloat16),
        carrier.astype(np.float32),
        low.astype(np.float32),
        high.astype(np.float32),
        start.astype(np.float32),
    )


def lane_ids(rows):
    return lax.broadcasted_iota(jnp.int32, (rows, LANES), 1)


def mirror_matrix():
    row = lax.broadcasted_iota(jnp.int32, (MIRROR, MIRROR), 0)
    col = lax.broadcasted_iota(jnp.int32, (MIRROR, MIRROR), 1)
    return jnp.where(row + col == MIRROR - 1, 1.0, 0.0).astype(jnp.bfloat16)


def start_copies(pairs, sems):
    copies = [pltpu.make_async_copy(src, dst, sems.at[n]) for n, (src, dst) in enumerate(pairs)]
    for copy in copies:
        copy.start()
    return copies


def high_turns(high, start):
    cos_s, sin_s = start[0:1], start[1:2]
    return high[0] * cos_s - high[1] * sin_s, high[0] * sin_s + high[1] * cos_s


def owners_of(pairs_from, upper):
    count = pairs_from // HALF
    if upper:
        return BAND // HALF + count, BAND // HALF + count + 1
    return BAND // HALF - 1 - count, BAND // HALF - 2 - count


def forward_kernel(
    x_hbm, table_hbm, carrier_hbm, low_hbm, high_hbm, start_hbm, out_ref,
    x_ref, table_ref, carrier_ref, low_ref, high_ref, start_ref, even_ref, odd_ref, product_ref, sems,
):
    chan_dev, time_dev = x_ref.shape
    highs = high_ref.shape[1]
    rows_all = time_dev // INNER * chan_dev
    span = LOW * chan_dev
    chunks = BAND // CHUNK
    pairs = [(x_hbm, x_ref), (carrier_hbm, carrier_ref), (table_hbm.at[0], table_ref.at[0])]
    pairs += [(low_hbm, low_ref), (high_hbm, high_ref), (start_hbm.at[lax.axis_index("tm")], start_ref)]
    pairs += [(table_hbm.at[n], table_ref.at[n]) for n in range(1, chunks)]
    copies = start_copies(pairs, sems)
    mirror = mirror_matrix()
    copies[0].wait()
    copies[1].wait()
    sides = []
    for side in range(2):
        sides.append(
            jnp.concatenate(
                [
                    x_ref[:, pl.ds(b * INNER + side * SIDE, SIDE)].astype(jnp.float32)
                    for b in range(time_dev // INNER)
                ],
                axis=0,
            )
        )
    first = sides[0].astype(jnp.bfloat16)
    before = jnp.concatenate(
        [
            jnp.dot(
                first[:, m * MIRROR : (m + 1) * MIRROR], mirror, preferred_element_type=jnp.float32
            )
            for m in reversed(range(SIDE // MIRROR))
        ],
        axis=1,
    )
    total = sides[1] + before
    change = sides[1] - before
    carrier_cos = carrier_ref[0:1, :]
    carrier_sin = carrier_ref[1:2, :]
    even_ref[:rows_all, :] = (total * carrier_cos).astype(jnp.bfloat16)
    even_ref[rows_all:, :] = (change * carrier_sin).astype(jnp.bfloat16)
    odd_ref[:rows_all, :] = (change * carrier_cos).astype(jnp.bfloat16)
    odd_ref[rows_all:, :] = (total * carrier_sin).astype(jnp.bfloat16)
    lane = lane_ids(chan_dev)

    def multiply(n):
        copies[2 if n == 0 else 5 + n].wait()
        product_ref[n % 2, :, :CHUNK] = jnp.dot(
            even_ref[...], table_ref[n, :, :CHUNK], preferred_element_type=jnp.float32
        )
        product_ref[n % 2, :, CHUNK:] = jnp.dot(
            odd_ref[...], table_ref[n, :, CHUNK:], preferred_element_type=jnp.float32
        )

    multiply(0)
    for copy in copies[3:6]:
        copy.wait()
    for n in range(chunks):
        if n + 1 < chunks:
            multiply(n + 1)
        for tile in range(CHUNK // LANES):
            cols = pl.ds(tile * LANES, LANES)
            sin_cols = pl.ds(CHUNK + tile * LANES, LANES)
            begin = n * CHUNK + tile * LANES
            lanes = (pl.ds(begin, LANES), pl.ds(BAND + begin, LANES))
            high_turn = [high_turns(high_ref[:, :, part], start_ref[:, part]) for part in lanes]
            real, imag = [None, None], [None, None]
            for h in range(highs):
                part_real, part_imag = [None, None], [None, None]
                for b in range(LOW):
                    row = h * span + b * chan_dev
                    rows = pl.ds(row, chan_dev)
                    more = pl.ds(rows_all + row, chan_dev)
                    even_cos = product_ref[n % 2, rows, cols]
                    odd_cos = product_ref[n % 2, more, cols]
                    odd_sin = product_ref[n % 2, rows, sin_cols]
                    even_sin = product_ref[n % 2, more, sin_cols]
                    parts = (
                        (even_cos - even_sin, odd_cos + odd_sin),
                        (even_cos + even_sin, odd_cos - odd_sin),
                    )
                    for half, (by_cos, by_sin) in enumerate(parts):
                        cos_b = low_ref[0, pl.ds(b, 1), lanes[half]]
                        sin_b = low_ref[1, pl.ds(b, 1), lanes[half]]
                        re = by_cos * cos_b - by_sin * sin_b
                        im = by_cos * sin_b + by_sin * cos_b
                        part_real[half] = re if b == 0 else part_real[half] + re
                        part_imag[half] = im if b == 0 else part_imag[half] + im
                for half in range(2):
                    cos_h = high_turn[half][0][h : h + 1]
                    sin_h = high_turn[half][1][h : h + 1]
                    re = part_real[half] * cos_h - part_imag[half] * sin_h
                    im = part_real[half] * sin_h + part_imag[half] * cos_h
                    real[half] = re if h == 0 else real[half] + re
                    imag[half] = im if h == 0 else imag[half] + im
            for half in range(2):
                re, im = real[half], -imag[half]
                one, two = owners_of(begin, half == 0)
                out_ref[one] = jnp.where(lane < HALF, re, pltpu.roll(im, HALF, 1)).astype(
                    out_ref.dtype
                )
                out_ref[two] = jnp.where(lane < HALF, pltpu.roll(re, HALF, 1), im).astype(
                    out_ref.dtype
                )


def forward(x, table, carrier, low, high, start):
    chan_dev, time_dev = x.shape
    rows = time_dev // INNER * chan_dev
    hbm = pl.BlockSpec(memory_space=pltpu.HBM)
    return pl.pallas_call(
        forward_kernel,
        in_specs=[hbm] * 6,
        out_specs=pl.BlockSpec(memory_space=pltpu.VMEM),
        scratch_shapes=[
            pltpu.VMEM(x.shape, x.dtype),
            pltpu.VMEM(table.shape, table.dtype),
            pltpu.VMEM(carrier.shape, carrier.dtype),
            pltpu.VMEM(low.shape, low.dtype),
            pltpu.VMEM(high.shape, high.dtype),
            pltpu.VMEM(start.shape[1:], start.dtype),
            pltpu.VMEM((2 * rows, SIDE), jnp.bfloat16),
            pltpu.VMEM((2 * rows, SIDE), jnp.bfloat16),
            pltpu.VMEM((2, 2 * rows, 2 * CHUNK), jnp.float32),
            pltpu.SemaphoreType.DMA((BAND // CHUNK + 5,)),
        ],
        out_shape=jax.ShapeDtypeStruct((MODES // HALF, chan_dev, LANES), jnp.bfloat16),
        cost_estimate=pl.CostEstimate(
            flops=2 * chan_dev * time_dev * MODES, bytes_accessed=4 << 20, transcendentals=0
        ),
        name="forward_modes",
    )(x, table, carrier, low, high, start)


def inverse_kernel(
    mixed_ref, table_hbm, carrier_ref, low_ref, high_ref, starts_ref, out_ref,
    table_ref, even_ref, odd_ref, cos_ref, sin_ref, sems,
):
    chan_dev, time_dev = out_ref.shape
    highs = high_ref.shape[1]
    rows_all = time_dev // INNER * chan_dev
    span = LOW * chan_dev
    chunks = BAND // CHUNK
    copies = start_copies([(table_hbm.at[n], table_ref.at[n]) for n in range(chunks)], sems)
    time_index = lax.axis_index("tm")
    lane = lane_ids(chan_dev)

    def turn(n):
        for tile in range(CHUNK // LANES):
            cols = pl.ds(tile * LANES, LANES)
            begin = n * CHUNK + tile * LANES
            lanes = (pl.ds(begin, LANES), pl.ds(BAND + begin, LANES))
            high_turn = [
                high_turns(high_ref[:, :, part], starts_ref[time_index, :, part]) for part in lanes
            ]
            modes = []
            for half in range(2):
                one, two = owners_of(begin, half == 0)
                first = mixed_ref[one].astype(jnp.float32)
                second = mixed_ref[two].astype(jnp.float32)
                modes.append(
                    (
                        jnp.where(lane < HALF, first, pltpu.roll(second, HALF, 1)),
                        jnp.where(lane < HALF, pltpu.roll(first, HALF, 1), second),
                    )
                )
            for h in range(highs):
                turned_h = []
                for half, (real, imag) in enumerate(modes):
                    cos_h = high_turn[half][0][h : h + 1]
                    sin_h = high_turn[half][1][h : h + 1]
                    turned_h.append((real * cos_h - imag * sin_h, real * sin_h + imag * cos_h))
                for b in range(0, LOW, 2):
                    row = h * span + b * chan_dev
                    rows = pl.ds(row, 2 * chan_dev)
                    more = pl.ds(rows_all + row, 2 * chan_dev)
                    parts = ([], [], [], [])
                    for c in (b, b + 1):
                        turned = []
                        for half, (real, imag) in enumerate(turned_h):
                            cos_b = low_ref[0, pl.ds(c, 1), lanes[half]]
                            sin_b = low_ref[1, pl.ds(c, 1), lanes[half]]
                            turned.append((real * cos_b - imag * sin_b, real * sin_b + imag * cos_b))
                        (up_re, up_im), (down_re, down_im) = turned
                        parts[0].append(up_re + down_re)
                        parts[1].append(up_im + down_im)
                        parts[2].append(up_re - down_re)
                        parts[3].append(up_im - down_im)
                    even_re, even_im, odd_re, odd_im = [
                        jnp.concatenate(part, axis=0).astype(jnp.bfloat16) for part in parts
                    ]
                    even_ref[n % 2, rows, cols] = even_re
                    even_ref[n % 2, more, cols] = even_im
                    odd_ref[n % 2, rows, cols] = odd_re
                    odd_ref[n % 2, more, cols] = odd_im

    turn(0)
    for n in range(chunks):
        copies[n].wait()
        by_cos = jnp.dot(
            even_ref[n % 2], table_ref[n, :CHUNK, :], preferred_element_type=jnp.float32
        )
        by_sin = jnp.dot(odd_ref[n % 2], table_ref[n, CHUNK:, :], preferred_element_type=jnp.float32)
        if n == 0:
            cos_ref[...] = by_cos
            sin_ref[...] = by_sin
        else:
            cos_ref[...] += by_cos
            sin_ref[...] += by_sin
        if n + 1 < chunks:
            turn(n + 1)
    even_re = cos_ref[:rows_all, :]
    even_im = cos_ref[rows_all:, :]
    odd_re = sin_ref[:rows_all, :]
    odd_im = sin_ref[rows_all:, :]
    carrier_cos = carrier_ref[0:1, :]
    carrier_sin = carrier_ref[1:2, :]
    after = carrier_cos * (even_re - odd_im) - carrier_sin * (even_im + odd_re)
    mirrored = carrier_cos * (even_re + odd_im) + carrier_sin * (even_im - odd_re)
    mirror = mirror_matrix()
    upper = mirrored.astype(jnp.bfloat16)
    lower = (mirrored - upper.astype(jnp.float32)).astype(jnp.bfloat16)
    pieces = []
    for n in reversed(range(SIDE // MIRROR)):
        cols = slice(n * MIRROR, (n + 1) * MIRROR)
        piece = jnp.dot(upper[:, cols], mirror, preferred_element_type=jnp.float32)
        pieces.append(piece + jnp.dot(lower[:, cols], mirror, preferred_element_type=jnp.float32))
    before = jnp.concatenate(pieces, axis=1)
    for b in range(highs * LOW):
        rows = slice(b * chan_dev, (b + 1) * chan_dev)
        out_ref[:, pl.ds(b * INNER, SIDE)] = before[rows]
        out_ref[:, pl.ds(b * INNER + SIDE, SIDE)] = after[rows]


def inverse(mixed, table, carrier, low, high, start, time_dev):
    owners, chan_dev, _ = mixed.shape
    rows = time_dev // INNER * chan_dev
    hbm = pl.BlockSpec(memory_space=pltpu.HBM)
    vmem = pl.BlockSpec(memory_space=pltpu.VMEM)
    return pl.pallas_call(
        inverse_kernel,
        in_specs=[vmem, hbm, vmem, vmem, vmem, vmem],
        out_specs=pl.BlockSpec(memory_space=pltpu.VMEM),
        scratch_shapes=[
            pltpu.VMEM(table.shape, table.dtype),
            pltpu.VMEM((2, 2 * rows, CHUNK), jnp.bfloat16),
            pltpu.VMEM((2, 2 * rows, CHUNK), jnp.bfloat16),
            pltpu.VMEM((2 * rows, SIDE), jnp.float32),
            pltpu.VMEM((2 * rows, SIDE), jnp.float32),
            pltpu.SemaphoreType.DMA((BAND // CHUNK,)),
        ],
        out_shape=jax.ShapeDtypeStruct((chan_dev, time_dev), jnp.float32),
        compiler_params=pltpu.CompilerParams(vmem_limit_bytes=VMEM_LIMIT),
        cost_estimate=pl.CostEstimate(
            flops=2 * chan_dev * time_dev * MODES, bytes_accessed=4 << 20, transcendentals=0
        ),
        name="inverse_modes",
    )(mixed, table, carrier, low, high, start)


def mix_kernel(spec_ref, weight_ref, out_ref, turned_ref, mixed_ref, *, steps_all):
    time_index = lax.axis_index("tm")
    chan_index = lax.axis_index("chan")
    turned_ref[...] = spec_ref[...].astype(jnp.float32).T
    mixed_ref[...] = jnp.zeros_like(mixed_ref)
    block_modes = weight_ref.shape[0]
    for m in range(block_modes):
        mode = chan_index * block_modes + m
        place = jnp.where(time_index * HALF < BAND, HALF - 1 - mode, mode)
        re_row = turned_ref[pl.ds(place, 1), :]
        im_row = turned_ref[pl.ds(HALF + place, 1), :]
        both = jnp.concatenate([re_row, im_row, jnp.zeros((6, LANES), jnp.float32)], axis=0).astype(
            jnp.bfloat16
        )
        by_real = jnp.dot(both, weight_ref[m, 0], preferred_element_type=jnp.float32)
        by_imag = jnp.dot(both, weight_ref[m, 1], preferred_element_type=jnp.float32)
        scale = jnp.where(time_index * HALF + mode == 0, 1.0 / steps_all, 2.0 / steps_all)
        mixed_ref[pl.ds(place, 1), :] = (by_real[0:1] - by_imag[1:2]) * scale
        mixed_ref[pl.ds(HALF + place, 1), :] = (by_imag[0:1] + by_real[1:2]) * scale
    out_ref[...] = mixed_ref[...].T.astype(out_ref.dtype)


def mix(spec, weight, steps_all):
    return pl.pallas_call(
        lambda *refs: mix_kernel(*refs, steps_all=steps_all),
        in_specs=[pl.BlockSpec(memory_space=pltpu.VMEM)] * 2,
        out_specs=pl.BlockSpec(memory_space=pltpu.VMEM),
        scratch_shapes=[pltpu.VMEM((128, LANES), jnp.float32), pltpu.VMEM((128, LANES), jnp.float32)],
        out_shape=jax.ShapeDtypeStruct(spec.shape, jnp.bfloat16),
        compiler_params=pltpu.CompilerParams(vmem_limit_bytes=4 << 20),
        name="mix_modes",
    )(spec, weight)


def output_kernel(weight_ref, bias_ref, spectral_ref, x_hbm, out_hbm, x_ref, out_ref, sems, out_sems):
    chan_dev, time_dev = out_ref.shape
    parts = x_ref.shape[0]
    width = time_dev // parts
    half = width // 2
    copies = start_copies(
        [(x_hbm.at[:, pl.ds(n * width, width)], x_ref.at[n]) for n in range(parts)], sems
    )
    weight = weight_ref[...].astype(jnp.float32)
    none = jnp.zeros_like(weight)
    stacked = jnp.concatenate(
        [jnp.concatenate([weight, none], axis=1), jnp.concatenate([none, weight], axis=1)], axis=0
    ).astype(jnp.bfloat16)
    diagonal = lax.broadcasted_iota(jnp.int32, (chan_dev, chan_dev), 0) == lax.broadcasted_iota(
        jnp.int32, (chan_dev, chan_dev), 1
    )
    bias = jnp.sum(jnp.where(diagonal, bias_ref[...], 0.0), axis=1, keepdims=True)
    results = []
    for n in range(parts):
        copies[n].wait()
        x = jnp.concatenate([x_ref[n, :, :half], x_ref[n, :, half:]], axis=0)
        skip = jnp.dot(stacked, x, preferred_element_type=jnp.float32)
        for side in range(2):
            cols = pl.ds(n * width + side * half, half)
            total = spectral_ref[:, cols] + skip[side * chan_dev : (side + 1) * chan_dev] + bias
            gelu = 0.5 * total * (1.0 + lax.erf(total * math.sqrt(0.5)))
            out_ref[:, cols] = gelu.astype(out_ref.dtype)
        cols = pl.ds(n * width, width)
        result = pltpu.make_async_copy(out_ref.at[:, cols], out_hbm.at[:, cols], out_sems.at[n])
        result.start()
        results.append(result)
    for result in results:
        result.wait()


def output(weight, bias, spectral, x):
    chan_dev, time_dev = spectral.shape
    parts = 8
    vmem = pl.BlockSpec(memory_space=pltpu.VMEM)
    hbm = pl.BlockSpec(memory_space=pltpu.HBM)
    return pl.pallas_call(
        output_kernel,
        in_specs=[vmem, vmem, vmem, hbm],
        out_specs=hbm,
        scratch_shapes=[
            pltpu.VMEM((parts, x.shape[0], time_dev // parts), x.dtype),
            pltpu.VMEM((chan_dev, time_dev), jnp.bfloat16),
            pltpu.SemaphoreType.DMA((parts,)),
            pltpu.SemaphoreType.DMA((parts,)),
        ],
        out_shape=jax.ShapeDtypeStruct((chan_dev, time_dev), jnp.bfloat16),
        compiler_params=pltpu.CompilerParams(vmem_limit_bytes=VMEM_LIMIT),
        cost_estimate=pl.CostEstimate(
            flops=2 * 2 * chan_dev * x.shape[0] * time_dev, bytes_accessed=10 << 20, transcendentals=0
        ),
        name="skip_and_output",
    )(weight, bias, spectral, x)


def sum_and_copy(arrived, copies):
    total = jnp.sum(arrived.astype(jnp.float32), axis=0).astype(jnp.bfloat16)
    return jnp.broadcast_to(total[None], (copies, *total.shape))


def shards(records, spectral_weight, skip_weight, skip_bias):
    groups, chan_dev, time_dev = records.shape
    tm_count = lax.axis_size("tm")
    chan_count = lax.axis_size("chan")
    steps_all = time_dev * tm_count
    forward_table, inverse_table, carrier, low, high, start = tables(steps_all, time_dev)
    x = records.reshape(chan_dev, time_dev)

    gathered = lax.all_gather(x, "chan", axis=0, tiled=True)

    partial = forward(x, forward_table, carrier, low, high, start)
    arrived = lax.all_to_all(partial, "tm", 0, 0, tiled=True)
    spectrum = sum_and_copy(arrived, chan_count)
    spectrum = lax.all_to_all(spectrum, "chan", 0, 0, tiled=True)
    mixed = mix(spectrum.reshape(-1, LANES), spectral_weight, steps_all)
    mixed = lax.all_to_all(mixed.reshape(spectrum.shape), "chan", 0, 0, tiled=True)
    mixed = sum_and_copy(mixed, tm_count)
    mixed = lax.all_to_all(mixed, "tm", 0, 0, tiled=True)
    spectral = inverse(mixed, inverse_table, carrier, low, high, start, time_dev)

    out = output(skip_weight, skip_bias[None, :], spectral, gathered)
    return out.reshape(groups, chan_dev, time_dev)


def solution(mesh):
    return jax.shard_map(
        shards,
        mesh=mesh,
        in_specs=(
            P(None, "chan", "tm"),
            P(("tm", "chan"), None, None, None),
            P("chan", None),
            P("chan"),
        ),
        out_specs=P(None, "chan", "tm"),
        check_vma=False,
    )
```

```python
import math

import jax
import jax.numpy as jnp
import numpy as np
from jax import lax
from jax.experimental import pallas as pl
from jax.experimental.pallas import tpu as pltpu
from jax.sharding import PartitionSpec as P

MODES = 2048
INNER = 2048
SIDE = INNER // 2
MIRROR = 256
BAND = MODES // 2
CHUNK = 256
LANES = 128
HALF = 64
VMEM_LIMIT = 52 << 20


def tables(steps_all, time_dev):
    tm_count = steps_all // time_dev
    blocks = time_dev // INNER
    pair = np.arange(BAND, dtype=np.int64)
    modes = np.concatenate([BAND + pair, BAND - 1 - pair])
    inner = 2 * np.arange(SIDE, dtype=np.int64) + 1

    def turn(half_steps, half_modes):
        angle = half_steps[:, None] * half_modes[None, :] % (4 * steps_all)
        return np.cos(angle * (math.pi / (2 * steps_all))), np.sin(angle * (math.pi / (2 * steps_all)))

    inner_cos, inner_sin = turn(inner, 2 * pair + 1)
    split = lambda a: a.reshape(SIDE, BAND // CHUNK, CHUNK).transpose(1, 0, 2)
    forward = np.concatenate([split(inner_cos), split(inner_sin)], axis=2)
    carrier = np.stack(turn(inner, np.array([2 * BAND - 1])))[:, :, 0]
    block = np.stack(turn(np.arange(blocks, dtype=np.int64) * (2 * INNER) + INNER - 1, 2 * modes))
    start = np.stack(turn(np.arange(tm_count, dtype=np.int64) * (2 * time_dev), 2 * modes), axis=1)
    return (
        np.ascontiguousarray(forward).astype(jnp.bfloat16),
        np.ascontiguousarray(forward.transpose(0, 2, 1)).astype(jnp.bfloat16),
        carrier.astype(np.float32),
        block.astype(np.float32),
        start.astype(np.float32),
    )


def lane_ids(rows):
    return lax.broadcasted_iota(jnp.int32, (rows, LANES), 1)


def mirror_matrix():
    row = lax.broadcasted_iota(jnp.int32, (MIRROR, MIRROR), 0)
    col = lax.broadcasted_iota(jnp.int32, (MIRROR, MIRROR), 1)
    return jnp.where(row + col == MIRROR - 1, 1.0, 0.0).astype(jnp.bfloat16)


def start_copies(pairs, sems):
    copies = [pltpu.make_async_copy(src, dst, sems.at[n]) for n, (src, dst) in enumerate(pairs)]
    for copy in copies:
        copy.start()
    return copies


def owners_of(pairs_from, upper):
    count = pairs_from // HALF
    if upper:
        return BAND // HALF + count, BAND // HALF + count + 1
    return BAND // HALF - 1 - count, BAND // HALF - 2 - count


def forward_kernel(
    x_hbm, table_hbm, carrier_hbm, block_hbm, start_hbm, out_ref,
    x_ref, table_ref, carrier_ref, block_ref, start_ref, even_ref, odd_ref, product_ref, sems,
):
    chan_dev, time_dev = x_ref.shape
    blocks = block_ref.shape[1]
    rows_all = time_dev // INNER * chan_dev
    chunks = BAND // CHUNK
    pairs = [(x_hbm, x_ref), (carrier_hbm, carrier_ref), (table_hbm.at[0], table_ref.at[0])]
    pairs += [(block_hbm, block_ref), (start_hbm.at[lax.axis_index("tm")], start_ref)]
    pairs += [(table_hbm.at[n], table_ref.at[n]) for n in range(1, chunks)]
    copies = start_copies(pairs, sems)
    mirror = mirror_matrix()
    copies[0].wait()
    copies[1].wait()
    sides = []
    for side in range(2):
        sides.append(
            jnp.concatenate(
                [
                    x_ref[:, pl.ds(b * INNER + side * SIDE, SIDE)].astype(jnp.float32)
                    for b in range(time_dev // INNER)
                ],
                axis=0,
            )
        )
    first = sides[0].astype(jnp.bfloat16)
    before = jnp.concatenate(
        [
            jnp.dot(
                first[:, m * MIRROR : (m + 1) * MIRROR], mirror, preferred_element_type=jnp.float32
            )
            for m in reversed(range(SIDE // MIRROR))
        ],
        axis=1,
    )
    total = sides[1] + before
    change = sides[1] - before
    carrier_cos = carrier_ref[0:1, :]
    carrier_sin = carrier_ref[1:2, :]
    even_ref[:rows_all, :] = (total * carrier_cos).astype(jnp.bfloat16)
    even_ref[rows_all:, :] = (change * carrier_sin).astype(jnp.bfloat16)
    odd_ref[:rows_all, :] = (change * carrier_cos).astype(jnp.bfloat16)
    odd_ref[rows_all:, :] = (total * carrier_sin).astype(jnp.bfloat16)
    lane = lane_ids(chan_dev)

    def multiply(n):
        copies[2 if n == 0 else 4 + n].wait()
        product_ref[n % 2, :, :CHUNK] = jnp.dot(
            even_ref[...], table_ref[n, :, :CHUNK], preferred_element_type=jnp.float32
        )
        product_ref[n % 2, :, CHUNK:] = jnp.dot(
            odd_ref[...], table_ref[n, :, CHUNK:], preferred_element_type=jnp.float32
        )

    multiply(0)
    for copy in copies[3:5]:
        copy.wait()
    for n in range(chunks):
        if n + 1 < chunks:
            multiply(n + 1)
        for tile in range(CHUNK // LANES):
            cols = pl.ds(tile * LANES, LANES)
            sin_cols = pl.ds(CHUNK + tile * LANES, LANES)
            begin = n * CHUNK + tile * LANES
            lanes = (pl.ds(begin, LANES), pl.ds(BAND + begin, LANES))
            part_real, part_imag = [None, None], [None, None]
            for b in range(blocks):
                row = b * chan_dev
                rows = pl.ds(row, chan_dev)
                more = pl.ds(rows_all + row, chan_dev)
                even_cos = product_ref[n % 2, rows, cols]
                odd_cos = product_ref[n % 2, more, cols]
                odd_sin = product_ref[n % 2, rows, sin_cols]
                even_sin = product_ref[n % 2, more, sin_cols]
                parts = (
                    (even_cos - even_sin, odd_cos + odd_sin),
                    (even_cos + even_sin, odd_cos - odd_sin),
                )
                for half, (by_cos, by_sin) in enumerate(parts):
                    cos_b = block_ref[0, pl.ds(b, 1), lanes[half]]
                    sin_b = block_ref[1, pl.ds(b, 1), lanes[half]]
                    re = by_cos * cos_b - by_sin * sin_b
                    im = by_cos * sin_b + by_sin * cos_b
                    part_real[half] = re if b == 0 else part_real[half] + re
                    part_imag[half] = im if b == 0 else part_imag[half] + im
            real, imag = [], []
            for half in range(2):
                cos_s = start_ref[0:1, lanes[half]]
                sin_s = start_ref[1:2, lanes[half]]
                real.append(part_real[half] * cos_s - part_imag[half] * sin_s)
                imag.append(part_real[half] * sin_s + part_imag[half] * cos_s)
            for half in range(2):
                re, im = real[half], -imag[half]
                one, two = owners_of(begin, half == 0)
                out_ref[one] = jnp.where(lane < HALF, re, pltpu.roll(im, HALF, 1)).astype(
                    out_ref.dtype
                )
                out_ref[two] = jnp.where(lane < HALF, pltpu.roll(re, HALF, 1), im).astype(
                    out_ref.dtype
                )


def forward(x, table, carrier, block, start):
    chan_dev, time_dev = x.shape
    rows = time_dev // INNER * chan_dev
    hbm = pl.BlockSpec(memory_space=pltpu.HBM)
    return pl.pallas_call(
        forward_kernel,
        in_specs=[hbm] * 5,
        out_specs=pl.BlockSpec(memory_space=pltpu.VMEM),
        scratch_shapes=[
            pltpu.VMEM(x.shape, x.dtype),
            pltpu.VMEM(table.shape, table.dtype),
            pltpu.VMEM(carrier.shape, carrier.dtype),
            pltpu.VMEM(block.shape, block.dtype),
            pltpu.VMEM(start.shape[1:], start.dtype),
            pltpu.VMEM((2 * rows, SIDE), jnp.bfloat16),
            pltpu.VMEM((2 * rows, SIDE), jnp.bfloat16),
            pltpu.VMEM((2, 2 * rows, 2 * CHUNK), jnp.float32),
            pltpu.SemaphoreType.DMA((BAND // CHUNK + 4,)),
        ],
        out_shape=jax.ShapeDtypeStruct((MODES // HALF, chan_dev, LANES), jnp.bfloat16),
        cost_estimate=pl.CostEstimate(
            flops=2 * chan_dev * time_dev * MODES, bytes_accessed=4 << 20, transcendentals=0
        ),
        name="forward_modes",
    )(x, table, carrier, block, start)


def inverse_kernel(
    mixed_ref, table_hbm, carrier_ref, block_ref, starts_ref, out_ref,
    table_ref, even_ref, odd_ref, cos_ref, sin_ref, sems,
):
    chan_dev, time_dev = out_ref.shape
    blocks = block_ref.shape[1]
    rows_all = time_dev // INNER * chan_dev
    chunks = BAND // CHUNK
    copies = start_copies([(table_hbm.at[n], table_ref.at[n]) for n in range(chunks)], sems)
    time_index = lax.axis_index("tm")
    lane = lane_ids(chan_dev)

    def turn(n):
        for tile in range(CHUNK // LANES):
            cols = pl.ds(tile * LANES, LANES)
            begin = n * CHUNK + tile * LANES
            lanes = (pl.ds(begin, LANES), pl.ds(BAND + begin, LANES))
            modes = []
            for half in range(2):
                one, two = owners_of(begin, half == 0)
                first = mixed_ref[one].astype(jnp.float32)
                second = mixed_ref[two].astype(jnp.float32)
                modes.append(
                    (
                        jnp.where(lane < HALF, first, pltpu.roll(second, HALF, 1)),
                        jnp.where(lane < HALF, pltpu.roll(first, HALF, 1), second),
                    )
                )
            started = []
            for half, (real, imag) in enumerate(modes):
                cos_s = starts_ref[time_index, 0:1, lanes[half]]
                sin_s = starts_ref[time_index, 1:2, lanes[half]]
                started.append((real * cos_s - imag * sin_s, real * sin_s + imag * cos_s))
            for b in range(0, blocks, 2):
                row = b * chan_dev
                rows = pl.ds(row, 2 * chan_dev)
                more = pl.ds(rows_all + row, 2 * chan_dev)
                parts = ([], [], [], [])
                for c in (b, b + 1):
                    turned = []
                    for half, (real, imag) in enumerate(started):
                        cos_b = block_ref[0, pl.ds(c, 1), lanes[half]]
                        sin_b = block_ref[1, pl.ds(c, 1), lanes[half]]
                        turned.append((real * cos_b - imag * sin_b, real * sin_b + imag * cos_b))
                    (up_re, up_im), (down_re, down_im) = turned
                    parts[0].append(up_re + down_re)
                    parts[1].append(up_im + down_im)
                    parts[2].append(up_re - down_re)
                    parts[3].append(up_im - down_im)
                even_re, even_im, odd_re, odd_im = [
                    jnp.concatenate(part, axis=0).astype(jnp.bfloat16) for part in parts
                ]
                even_ref[n % 2, rows, cols] = even_re
                even_ref[n % 2, more, cols] = even_im
                odd_ref[n % 2, rows, cols] = odd_re
                odd_ref[n % 2, more, cols] = odd_im

    turn(0)
    for n in range(chunks):
        copies[n].wait()
        by_cos = jnp.dot(
            even_ref[n % 2], table_ref[n, :CHUNK, :], preferred_element_type=jnp.float32
        )
        by_sin = jnp.dot(odd_ref[n % 2], table_ref[n, CHUNK:, :], preferred_element_type=jnp.float32)
        if n == 0:
            cos_ref[...] = by_cos
            sin_ref[...] = by_sin
        else:
            cos_ref[...] += by_cos
            sin_ref[...] += by_sin
        if n + 1 < chunks:
            turn(n + 1)
    even_re = cos_ref[:rows_all, :]
    even_im = cos_ref[rows_all:, :]
    odd_re = sin_ref[:rows_all, :]
    odd_im = sin_ref[rows_all:, :]
    carrier_cos = carrier_ref[0:1, :]
    carrier_sin = carrier_ref[1:2, :]
    after = carrier_cos * (even_re - odd_im) - carrier_sin * (even_im + odd_re)
    mirrored = carrier_cos * (even_re + odd_im) + carrier_sin * (even_im - odd_re)
    mirror = mirror_matrix()
    upper = mirrored.astype(jnp.bfloat16)
    lower = (mirrored - upper.astype(jnp.float32)).astype(jnp.bfloat16)
    pieces = []
    for n in reversed(range(SIDE // MIRROR)):
        cols = slice(n * MIRROR, (n + 1) * MIRROR)
        piece = jnp.dot(upper[:, cols], mirror, preferred_element_type=jnp.float32)
        pieces.append(piece + jnp.dot(lower[:, cols], mirror, preferred_element_type=jnp.float32))
    before = jnp.concatenate(pieces, axis=1)
    for b in range(blocks):
        rows = slice(b * chan_dev, (b + 1) * chan_dev)
        out_ref[:, pl.ds(b * INNER, SIDE)] = before[rows]
        out_ref[:, pl.ds(b * INNER + SIDE, SIDE)] = after[rows]


def inverse(mixed, table, carrier, block, start, time_dev):
    owners, chan_dev, _ = mixed.shape
    rows = time_dev // INNER * chan_dev
    hbm = pl.BlockSpec(memory_space=pltpu.HBM)
    vmem = pl.BlockSpec(memory_space=pltpu.VMEM)
    return pl.pallas_call(
        inverse_kernel,
        in_specs=[vmem, hbm, vmem, vmem, vmem],
        out_specs=pl.BlockSpec(memory_space=pltpu.VMEM),
        scratch_shapes=[
            pltpu.VMEM(table.shape, table.dtype),
            pltpu.VMEM((2, 2 * rows, CHUNK), jnp.bfloat16),
            pltpu.VMEM((2, 2 * rows, CHUNK), jnp.bfloat16),
            pltpu.VMEM((2 * rows, SIDE), jnp.float32),
            pltpu.VMEM((2 * rows, SIDE), jnp.float32),
            pltpu.SemaphoreType.DMA((BAND // CHUNK,)),
        ],
        out_shape=jax.ShapeDtypeStruct((chan_dev, time_dev), jnp.float32),
        compiler_params=pltpu.CompilerParams(vmem_limit_bytes=VMEM_LIMIT),
        cost_estimate=pl.CostEstimate(
            flops=2 * chan_dev * time_dev * MODES, bytes_accessed=4 << 20, transcendentals=0
        ),
        name="inverse_modes",
    )(mixed, table, carrier, block, start)


def mix_kernel(spec_ref, weight_ref, out_ref, turned_ref, mixed_ref, *, steps_all):
    time_index = lax.axis_index("tm")
    chan_index = lax.axis_index("chan")
    turned_ref[...] = spec_ref[...].astype(jnp.float32).T
    mixed_ref[...] = jnp.zeros_like(mixed_ref)
    block_modes = weight_ref.shape[0]
    for m in range(block_modes):
        mode = chan_index * block_modes + m
        place = jnp.where(time_index * HALF < BAND, HALF - 1 - mode, mode)
        re_row = turned_ref[pl.ds(place, 1), :]
        im_row = turned_ref[pl.ds(HALF + place, 1), :]
        both = jnp.concatenate([re_row, im_row, jnp.zeros((6, LANES), jnp.float32)], axis=0).astype(
            jnp.bfloat16
        )
        by_real = jnp.dot(both, weight_ref[m, 0], preferred_element_type=jnp.float32)
        by_imag = jnp.dot(both, weight_ref[m, 1], preferred_element_type=jnp.float32)
        scale = jnp.where(time_index * HALF + mode == 0, 1.0 / steps_all, 2.0 / steps_all)
        mixed_ref[pl.ds(place, 1), :] = (by_real[0:1] - by_imag[1:2]) * scale
        mixed_ref[pl.ds(HALF + place, 1), :] = (by_imag[0:1] + by_real[1:2]) * scale
    out_ref[...] = mixed_ref[...].T.astype(out_ref.dtype)


def mix(spec, weight, steps_all):
    return pl.pallas_call(
        lambda *refs: mix_kernel(*refs, steps_all=steps_all),
        in_specs=[pl.BlockSpec(memory_space=pltpu.VMEM)] * 2,
        out_specs=pl.BlockSpec(memory_space=pltpu.VMEM),
        scratch_shapes=[pltpu.VMEM((128, LANES), jnp.float32), pltpu.VMEM((128, LANES), jnp.float32)],
        out_shape=jax.ShapeDtypeStruct(spec.shape, jnp.bfloat16),
        compiler_params=pltpu.CompilerParams(vmem_limit_bytes=4 << 20),
        name="mix_modes",
    )(spec, weight)


def output_kernel(weight_ref, bias_ref, spectral_ref, x_hbm, out_hbm, x_ref, out_ref, sems, out_sems):
    chan_dev, time_dev = out_ref.shape
    parts = x_ref.shape[0]
    width = time_dev // parts
    half = width // 2
    copies = start_copies(
        [(x_hbm.at[:, pl.ds(n * width, width)], x_ref.at[n]) for n in range(parts)], sems
    )
    weight = weight_ref[...].astype(jnp.float32)
    none = jnp.zeros_like(weight)
    stacked = jnp.concatenate(
        [jnp.concatenate([weight, none], axis=1), jnp.concatenate([none, weight], axis=1)], axis=0
    ).astype(jnp.bfloat16)
    diagonal = lax.broadcasted_iota(jnp.int32, (chan_dev, chan_dev), 0) == lax.broadcasted_iota(
        jnp.int32, (chan_dev, chan_dev), 1
    )
    bias = jnp.sum(jnp.where(diagonal, bias_ref[...], 0.0), axis=1, keepdims=True)
    results = []
    for n in range(parts):
        copies[n].wait()
        x = jnp.concatenate([x_ref[n, :, :half], x_ref[n, :, half:]], axis=0)
        skip = jnp.dot(stacked, x, preferred_element_type=jnp.float32)
        for side in range(2):
            cols = pl.ds(n * width + side * half, half)
            total = spectral_ref[:, cols] + skip[side * chan_dev : (side + 1) * chan_dev] + bias
            gelu = 0.5 * total * (1.0 + lax.erf(total * math.sqrt(0.5)))
            out_ref[:, cols] = gelu.astype(out_ref.dtype)
        cols = pl.ds(n * width, width)
        result = pltpu.make_async_copy(out_ref.at[:, cols], out_hbm.at[:, cols], out_sems.at[n])
        result.start()
        results.append(result)
    for result in results:
        result.wait()


def output(weight, bias, spectral, x):
    chan_dev, time_dev = spectral.shape
    parts = 8
    vmem = pl.BlockSpec(memory_space=pltpu.VMEM)
    hbm = pl.BlockSpec(memory_space=pltpu.HBM)
    return pl.pallas_call(
        output_kernel,
        in_specs=[vmem, vmem, vmem, hbm],
        out_specs=hbm,
        scratch_shapes=[
            pltpu.VMEM((parts, x.shape[0], time_dev // parts), x.dtype),
            pltpu.VMEM((chan_dev, time_dev), jnp.bfloat16),
            pltpu.SemaphoreType.DMA((parts,)),
            pltpu.SemaphoreType.DMA((parts,)),
        ],
        out_shape=jax.ShapeDtypeStruct((chan_dev, time_dev), jnp.bfloat16),
        compiler_params=pltpu.CompilerParams(vmem_limit_bytes=VMEM_LIMIT),
        cost_estimate=pl.CostEstimate(
            flops=2 * 2 * chan_dev * x.shape[0] * time_dev, bytes_accessed=10 << 20, transcendentals=0
        ),
        name="skip_and_output",
    )(weight, bias, spectral, x)


def sum_and_copy(arrived, copies):
    total = jnp.sum(arrived.astype(jnp.float32), axis=0).astype(jnp.bfloat16)
    return jnp.broadcast_to(total[None], (copies, *total.shape))


def shards(records, spectral_weight, skip_weight, skip_bias):
    groups, chan_dev, time_dev = records.shape
    tm_count = lax.axis_size("tm")
    chan_count = lax.axis_size("chan")
    steps_all = time_dev * tm_count
    forward_table, inverse_table, carrier, block, start = tables(steps_all, time_dev)
    x = records.reshape(chan_dev, time_dev)

    gathered = lax.all_gather(x, "chan", axis=0, tiled=True)

    partial = forward(x, forward_table, carrier, block, start)
    arrived = lax.all_to_all(partial, "tm", 0, 0, tiled=True)
    spectrum = sum_and_copy(arrived, chan_count)
    spectrum = lax.all_to_all(spectrum, "chan", 0, 0, tiled=True)
    mixed = mix(spectrum.reshape(-1, LANES), spectral_weight, steps_all)
    mixed = lax.all_to_all(mixed.reshape(spectrum.shape), "chan", 0, 0, tiled=True)
    mixed = sum_and_copy(mixed, tm_count)
    mixed = lax.all_to_all(mixed, "tm", 0, 0, tiled=True)
    spectral = inverse(mixed, inverse_table, carrier, block, start, time_dev)

    out = output(skip_weight, skip_bias[None, :], spectral, gathered)
    return out.reshape(groups, chan_dev, time_dev)


def solution(mesh):
    return jax.shard_map(
        shards,
        mesh=mesh,
        in_specs=(
            P(None, "chan", "tm"),
            P(("tm", "chan"), None, None, None),
            P("chan", None),
            P("chan"),
        ),
        out_specs=P(None, "chan", "tm"),
        check_vma=False,
    )
```
